32 devices in a mesh: pw: 4 (over y, core), band: 8 (over z, x).
Axes of the slice: x: 2, y: 2, z: 4, core: 2. Of those that a mesh axis runs over, the one named last changes fastest.
Arguments:
- psi: bfloat16 [2, 8, 24576], P(None, 'band', 'pw'), may hold values from -9 to 9
- gvec_index: int32 [24576], P('pw'), may hold values from 0 to 1769471, as said below
- vloc: float32 [192, 192, 192], P(None, 'pw'), may hold values from -3 to 1
- beta: bfloat16 [2, 72, 24576], P(None, None, 'pw'), may hold values from -0.15625 to 0.15625
- dmat: float32 [4, 18, 18], replicated, may hold values from -1 to 3
- qmat: float32 [4, 18, 18], replicated, may hold values from -1 to 2
Outputs:
- hpsi: bfloat16 [2, 8, 24576], P(None, 'band', 'pw')
- spsi: bfloat16 [2, 8, 24576], P(None, 'band', 'pw')
- gram: float32 [2, 8, 8], P(None, 'band')
The draws below stay inside these ranges and needn't reach their ends.
Inputs may be any that keep to these rules, and one draw needn't show every extreme that they name: `gvec_index`: each entry is (x - k * 48) * 192 * 192 + y * 192 + z for the grid cell (x, y, z) of its plane wave, where k is the entry's block of 6144 plane waves and x lies in k * 48 .. (k + 1) * 48 - 1; no cell appears twice.
All inputs are finite; a program needn't handle non-finite values.
Results may differ from the reference program's by a relative error of at most 0.0069.
Values may be sent and summed in bfloat16 or wider, within the bound.
No kernel may reach another device: no remote copies, remote signals or barrier semaphores. Data moves between devices by JAX's collectives and lax.ppermute only.
A program may use at most 128 MiB of HBM per device.

```python
import jax
import jax.numpy as jnp
from jax import lax

NG = 192
PROJ_ATOM = 18
ATOMS = 4
PW_DEV = 6144
PW = 24576
BANDS = 8
NPROJ = 72
N_PW = 4


def draw_psi(key, part):
    folded_key = jax.random.fold_in(key, 101)
    subkeys = jax.random.split(folded_key, 5)
    samples = jnp.clip(jax.random.normal(subkeys[0], (2, BANDS, PW), jnp.float32), -4.0, 4.0)
    first_order = jax.random.permutation(subkeys[1], BANDS)
    second_order = jax.random.permutation(subkeys[2], BANDS)
    first_weight = jax.random.uniform(subkeys[3], (BANDS,), jnp.float32, 0.3, 0.6)
    second_weight = jax.random.uniform(subkeys[4], (BANDS,), jnp.float32, 0.3, 0.6)
    blended = samples + first_weight[None, :, None] * samples[:, first_order] + second_weight[None, :, None] * samples[:, second_order]
    return blended.astype(jnp.bfloat16)


def draw_gvec_index(key, part):
    folded_key = jax.random.fold_in(key, 202)
    slab_cells = NG // N_PW * NG * NG

    def one_block(position):
        block_key = jax.random.fold_in(folded_key, position)
        inner = jax.random.permutation(jax.random.fold_in(block_key, 1), slab_cells - 2)[:PW_DEV - 2] + 1
        ends = jnp.array([0, slab_cells - 1], dtype=jnp.int32)
        full = jnp.concatenate([ends, inner.astype(jnp.int32)])
        order = jax.random.permutation(jax.random.fold_in(block_key, 2), PW_DEV)
        return full[order]
    blocks = jax.vmap(one_block)(jnp.arange(N_PW, dtype=jnp.int32))
    return blocks.reshape(-1).astype(jnp.int32)


def block_matrix(key, salt, lowest, highest, spread):
    subkeys = jax.random.split(jax.random.fold_in(key, salt), 2)
    diagonal = jax.random.uniform(subkeys[0], (ATOMS, PROJ_ATOM), jnp.float32, lowest, highest)
    coupling = jax.random.normal(subkeys[1], (ATOMS, PROJ_ATOM, PROJ_ATOM), jnp.float32) * spread
    coupling = 0.5 * (coupling + jnp.swapaxes(coupling, 1, 2))
    identity = jnp.eye(PROJ_ATOM, dtype=jnp.float32)
    return coupling * (1.0 - identity)[None] + diagonal[:, :, None] * identity[None]


def draw_dmat(key, part):
    return block_matrix(key, 303, 1.5, 3.0, 0.15)


def draw_qmat(key, part):
    return block_matrix(key, 404, 0.8, 1.6, 0.08)


def shard_levels(key, extent, cuts, smallest, high):
    def one(axis_at, parts):
        steps = jax.random.uniform(jax.random.fold_in(jax.random.fold_in(key, 6), axis_at), (parts,), jnp.float32, smallest / len(cuts), high / len(cuts))
        return jnp.repeat(jnp.exp(steps), extent[axis_at] // parts).reshape((-1,) + (1,) * (len(extent) - axis_at - 1))

    level = one(*cuts[0])
    for cut in cuts[1:]:
        level = level * one(*cut)
    return level


def normal_values(rng, shape, deviation, bound, cuts=(), kind=jnp.bfloat16):
    entries = jax.random.normal(rng, shape, jnp.float32) * deviation
    if len(cuts) > 0:
        entries = shard_levels(rng, shape, cuts, -0.22, 0.18) * entries
    return jnp.clip(entries, min=-bound, max=bound).astype(kind)


def setup_inputs(seed: int = 0) -> dict:
    seeds = jax.random.split(jax.random.key(seed), 7)
    psi = draw_psi(jax.random.fold_in(seeds[6], 71), 0)
    gvec_index = draw_gvec_index(jax.random.fold_in(seeds[6], 71), 0)
    vloc = jnp.clip(-3.0 + 4.0 * jax.random.uniform(seeds[2], (NG, NG, NG), jnp.float32) ** shard_levels(seeds[2], (NG, NG, NG), ((1, 4),), -0.2, 0.2), -3.0, 1.0)
    beta = normal_values(seeds[3], (2, NPROJ, PW), (PW_DEV * N_PW // 16) ** -0.5, 0.15625, ((2, 4),))
    dmat = draw_dmat(jax.random.fold_in(seeds[6], 71), 0)
    qmat = draw_qmat(jax.random.fold_in(seeds[6], 71), 0)
    return dict(psi=psi, gvec_index=gvec_index, vloc=vloc, beta=beta, dmat=dmat, qmat=qmat)


def dft_table(length, orient):
    counter = jnp.arange(length, dtype=jnp.int32)
    phase = counter[:, None] * counter[None, :] % length
    angle = phase.astype(jnp.float32) * (2.0 * jnp.pi / length)
    factor = 1.0 / jnp.sqrt(jnp.float32(length))
    cosine = jnp.cos(angle) * factor
    sine_part = orient * jnp.sin(angle) * factor
    upper = jnp.concatenate([cosine, sine_part], axis=1)
    lower = jnp.concatenate([-sine_part, cosine], axis=1)
    return jnp.concatenate([upper, lower], axis=0).astype(jnp.bfloat16)

def along_last(lattice, matrix):
    return jnp.dot(lattice.astype(jnp.float32), matrix.astype(jnp.float32), precision=lax.Precision.HIGHEST)

def along_middle(lattice, matrix):
    size_a, size_b, size_c = lattice.shape
    halfway = size_c // 2
    shaped = lattice.reshape(size_a, size_b, 2, halfway).astype(jnp.float32)
    square = matrix.reshape(2, halfway, 2, halfway).astype(jnp.float32)
    result = jnp.einsum('xypz,pyqk->xkqz', shaped, square, precision=lax.Precision.HIGHEST)
    return result.reshape(size_a, size_b, size_c)

def along_first(lattice, matrix):
    size_a, size_b, size_c = lattice.shape
    halfway = size_c // 2
    shaped = lattice.reshape(size_a, size_b, 2, halfway).astype(jnp.float32)
    square = matrix.reshape(2, halfway, 2, halfway).astype(jnp.float32)
    result = jnp.einsum('xypz,pxqk->kyqz', shaped, square, precision=lax.Precision.HIGHEST)
    return result.reshape(size_a, size_b, size_c)

def folded(level):
    return jnp.where(level < NG // 2, level, level - NG).astype(jnp.float32)

def pair_dot(left, right):
    return jnp.dot(left, right.T, preferred_element_type=jnp.float32)

def plain_dot(left, right):
    return jnp.dot(left, right, preferred_element_type=jnp.float32)

def reference(psi, gvec_index, vloc, beta, dmat, qmat):
    slab_cells = NG // N_PW * NG * NG
    owner = jnp.arange(PW, dtype=jnp.int32) // PW_DEV
    global_cell = (gvec_index + owner * slab_cells).astype(jnp.int32)
    row_index = global_cell // NG
    column = global_cell % NG
    place_re = (row_index * (2 * NG) + column).astype(jnp.int32)
    place_im = (place_re + NG).astype(jnp.int32)
    plus_table = dft_table(NG, 1.0)
    minus_table = dft_table(NG, -1.0)
    potential = vloc.astype(jnp.float32)[:, :, None, :]

    def local_term(coefs):
        lattice = jnp.zeros((NG * NG * 2 * NG,), jnp.bfloat16)
        lattice = lattice.at[place_re].set(coefs[0]).at[place_im].set(coefs[1])
        lattice = lattice.reshape(NG, NG, 2 * NG)
        lattice = along_last(lattice, plus_table).astype(jnp.bfloat16)
        lattice = along_middle(lattice, plus_table).astype(jnp.bfloat16)
        spatial = along_first(lattice, plus_table).reshape(NG, NG, 2, NG)
        lattice = (spatial * potential).reshape(NG, NG, 2 * NG).astype(jnp.bfloat16)
        lattice = along_first(lattice, minus_table).astype(jnp.bfloat16)
        lattice = along_middle(lattice, minus_table).astype(jnp.bfloat16)
        flat_out = along_last(lattice, minus_table).reshape(-1)
        return jnp.stack([flat_out[place_re], flat_out[place_im]])
    local = lax.map(local_term, jnp.transpose(psi, (1, 0, 2)))
    local = jnp.transpose(local, (1, 0, 2))
    plane_x = folded(global_cell // (NG * NG))
    plane_y = folded(global_cell // NG % NG)
    plane_z = folded(global_cell % NG)
    kinetic = 4.0 * (plane_x * plane_x + plane_y * plane_y + plane_z * plane_z) / (NG * NG)
    proj_re = pair_dot(psi[0], beta[0]) + pair_dot(psi[1], beta[1])
    proj_im = pair_dot(psi[1], beta[0]) - pair_dot(psi[0], beta[1])
    coef = jnp.stack([proj_re, proj_im]).reshape(2, BANDS, ATOMS, PROJ_ATOM)
    d_coef = jnp.einsum('aij,cbaj->cbai', dmat, coef, precision=lax.Precision.HIGHEST)
    d_coef = d_coef.reshape(2, BANDS, NPROJ).astype(jnp.bfloat16)
    q_coef = jnp.einsum('aij,cbaj->cbai', qmat, coef, precision=lax.Precision.HIGHEST)
    q_coef = q_coef.reshape(2, BANDS, NPROJ).astype(jnp.bfloat16)

    def expand(weights):
        real_part = plain_dot(weights[0], beta[0]) - plain_dot(weights[1], beta[1])
        imag_part = plain_dot(weights[0], beta[1]) + plain_dot(weights[1], beta[0])
        return jnp.stack([real_part, imag_part])
    psi_wide = psi.astype(jnp.float32)
    hpsi = (local + kinetic[None, None, :] * psi_wide + expand(d_coef)).astype(jnp.bfloat16)
    spsi = (psi_wide + expand(q_coef)).astype(jnp.bfloat16)
    gram_re = (pair_dot(psi[0], spsi[0]) + pair_dot(psi[1], spsi[1])) / PW
    gram_im = (pair_dot(psi[0], spsi[1]) - pair_dot(psi[1], spsi[0])) / PW
    return (hpsi, spsi, jnp.stack([gram_re, gram_im]))
```

```python
import functools

import jax
import jax.numpy as jnp
import ml_dtypes
import numpy as np
from jax import lax
from jax.experimental import pallas as pl
from jax.experimental.pallas import tpu as pltpu
from jax.sharding import PartitionSpec as P

LANES = 128
VMEM_LIMIT = 60 * 1024 * 1024


def round_up(value, unit):
    return -(-value // unit) * unit


def dft_parts(length):
    counter = np.arange(length)
    phase = counter[:, None] * counter[None, :] % length
    angle = phase.astype(np.float32) * np.float32(2.0 * np.pi / length)
    factor = np.float32(1.0) / np.sqrt(np.float32(length))
    return (np.cos(angle) * factor).astype(np.float32), (np.sin(angle) * factor).astype(np.float32)


def as_bf16(array):
    return np.asarray(array).astype(ml_dtypes.bfloat16)


def tables_of(length, planes, blocks):
    half = length // 2
    cosine, sine = dft_parts(length)
    rows = round_up(planes, 8)
    own = np.zeros((blocks, 2 * rows, length), np.float32)
    for block in range(blocks):
        span = slice(block * planes, (block + 1) * planes)
        own[block, :planes] = cosine[span]
        own[block, rows : rows + planes] = sine[span]
    along_z = np.stack([cosine, sine])

    def square(c, s):
        return np.block([[c, -s], [s, c]])

    along_x = np.stack(
        [
            square(cosine[:half, 0::2], sine[:half, 0::2]),
            square(cosine[:half, 1::2], sine[:half, 1::2]),
            square(cosine[0::2, :half], -sine[0::2, :half]),
            square(cosine[1::2, :half], -sine[1::2, :half]),
        ]
    )
    return as_bf16(own), as_bf16(along_z), as_bf16(along_x)


def cell_parts(index, length):
    cell = index.astype(jnp.float32)
    x = jnp.floor((cell + 0.5) * (1.0 / (length * length)))
    rest = cell - x * (length * length)
    y = jnp.floor((rest + 0.5) * (1.0 / length))
    return x, y, rest - y * length


def iota(shape, dim):
    return lax.broadcasted_iota(jnp.int32, shape, dim).astype(jnp.float32)


def where_bf16(mask, value):
    return jnp.where(mask, value, 0.0).astype(jnp.bfloat16)


def dot(left, right):
    return jnp.dot(left, right, preferred_element_type=jnp.float32)


def dot_lanes(left, right):
    return lax.dot_general(left, right, (((1,), (1,)), ((), ())), preferred_element_type=jnp.float32)


def group_kernel(length, planes, chunks, gvec_ref, psi_ref, pay_ref, slot_ref, hot, counts, spread, pick):
    waves = gvec_ref.shape[1]
    tiles = waves // LANES
    rows = round_up(planes, 16)
    x, y, z = cell_parts(gvec_ref[...], length)
    psi = psi_ref[...].astype(jnp.float32)
    plane = iota((rows, LANES), 0)
    for tile in range(tiles):
        span = slice(tile * LANES, (tile + 1) * LANES)
        hot[tile * rows : (tile + 1) * rows, :] = where_bf16(plane == x[:, span], 1.0)
    upto = jnp.where(iota((LANES, LANES), 0) <= iota((LANES, LANES), 1), 1.0, 0.0)
    upto = jnp.concatenate([upto, jnp.ones((LANES, LANES), jnp.float32)], axis=1)
    counts[...] = dot(hot[...], upto.astype(jnp.bfloat16))
    total = jnp.zeros((rows, LANES), jnp.float32)
    for tile in range(tiles):
        total = total + counts[tile * rows : (tile + 1) * rows, LANES:]
    need = jnp.maximum(jnp.floor((total + (LANES - 0.5)) * (1.0 / LANES)), 1.0)
    need = jnp.where(plane < planes, need, 0.0)
    below = where_bf16(iota((rows, rows), 1) < iota((rows, rows), 0), 1.0)
    first = dot(below, need.astype(jnp.bfloat16))
    ends = jnp.where((plane < planes) & (iota((rows, LANES), 1) >= first + need), 1.0, 0.0)
    chunk_plane = jnp.sum(ends, axis=0, keepdims=True)
    running = first * LANES - 1.0
    upper = iota((chunks, LANES), 0)
    lower = iota((LANES, LANES), 0)
    for tile in range(tiles):
        span = slice(tile * LANES, (tile + 1) * LANES)
        part = slice(tile * rows, (tile + 1) * rows)
        mine = plane == x[:, span]
        slot = jnp.where(mine, counts[part, :LANES] + running, 0.0)
        slot = jnp.sum(slot, axis=0, keepdims=True)
        running = running + counts[part, LANES:]
        slot_ref[:, span] = slot
        high = jnp.floor((slot + 0.5) * (1.0 / LANES))
        at_high = upper == high
        spread[0:chunks, span] = where_bf16(at_high, psi[0:1, span])
        spread[chunks : 2 * chunks, span] = where_bf16(at_high, psi[1:2, span])
        spread[2 * chunks : 3 * chunks, span] = where_bf16(at_high, y[:, span])
        spread[3 * chunks : 4 * chunks, span] = where_bf16(at_high, z[:, span])
        pick[:, span] = where_bf16(lower == slot - high * LANES, 1.0)
    pay_ref[0 : 4 * chunks, :] = dot_lanes(spread[...], pick[...]).astype(jnp.bfloat16)
    pay_ref[4 * chunks :, :] = jnp.broadcast_to(chunk_plane, (16, LANES)).astype(jnp.bfloat16)


def group_waves(index, psi, length, planes, chunks):
    waves = index.shape[1]
    rows = round_up(planes, 16)
    tiles = waves // LANES
    return pl.pallas_call(
        functools.partial(group_kernel, length, planes, chunks),
        out_shape=(
            jax.ShapeDtypeStruct((4 * chunks + 16, LANES), jnp.bfloat16),
            jax.ShapeDtypeStruct((1, waves), jnp.float32),
        ),
        scratch_shapes=[
            pltpu.VMEM((tiles * rows, LANES), jnp.bfloat16),
            pltpu.VMEM((tiles * rows, 2 * LANES), jnp.float32),
            pltpu.VMEM((4 * chunks, waves), jnp.bfloat16),
            pltpu.VMEM((LANES, waves), jnp.bfloat16),
        ],
        compiler_params=pltpu.CompilerParams(vmem_limit_bytes=VMEM_LIMIT),
        name="group_waves",
    )(index, psi)


def lattice_kernel(length, planes, chunks, blocks, *refs):
    pays = refs[:blocks]
    vloc_hbm, own_ref, along_z, along_x = refs[blocks : blocks + 4]
    outs = refs[blocks + 4 : 2 * blocks + 4]
    wide, cells_a, cells_b, phases, vloc, vloc_a, vloc_b, result, maps, maps_s, sems = refs[2 * blocks + 4 :]
    half = length // 2
    rows = round_up(planes, 8)
    both = 2 * rows
    spare = blocks * planes
    tail = length - LANES
    me = lax.axis_index("pw")
    load = pltpu.make_async_copy(vloc_hbm, vloc, sems.at[0])
    load.start()
    for s in range(blocks):
        maps[s * 8 : (s + 1) * 8, :] = pays[s][4 * chunks : 4 * chunks + 16, :].astype(jnp.int32)[:8]
    fetch = pltpu.make_async_copy(maps, maps_s, sems.at[1])
    fetch.start()
    for s in range(blocks):
        wide[s * 4 * chunks : (s + 1) * 4 * chunks, :] = pays[s][0 : 4 * chunks, :].astype(jnp.float32)
    own = own_ref[me]
    fetch.wait()
    used = jnp.int32(0)
    for s in range(blocks):
        used = jnp.maximum(used, lax.fori_loop(
            0, chunks, lambda c, n: n + jnp.where(maps_s[s * 8, c] < planes, 1, 0), jnp.int32(0)))
    level = iota((length, LANES), 0)
    group = 4 if blocks % 4 == 0 else 1

    def place(s, c):
        at = maps_s[s * 8, c]
        return jnp.where(at < planes, (me ^ s) * planes + at, spare)

    def row(s, part, c):
        return wide[pl.ds((s * 4 + part) * chunks + c, 1), :]

    def forward(c, _):
        for base in range(0, blocks, group):
            found = []
            for s in range(base, base + group):
                pick_y = where_bf16(level == row(s, 2, c), 1.0)
                phase = dot(own, pick_y)
                phases[s * chunks + c] = phase.astype(jnp.bfloat16)
                re, im = row(s, 0, c), row(s, 1, c)
                cos, sin = phase[:rows], phase[rows:]
                mixed = jnp.concatenate([re * cos - im * sin, re * sin + im * cos], axis=0)
                pick_z = where_bf16(level == row(s, 3, c), 1.0)
                part = dot_lanes(mixed.astype(jnp.bfloat16), pick_z)
                at = place(s, c)
                before = place(s, jnp.maximum(c - 1, 0))
                fresh = (c == 0) | (at != before)
                span = pl.ds(pl.multiple_of(at * both, 8), both)
                near = part[:, :LANES] + jnp.where(fresh, 0.0, cells_a[span, :])
                far = part[:, LANES:] + jnp.where(fresh, 0.0, cells_b[span, :tail])
                found.append((span, near, far))
            for span, near, far in found:
                cells_a[span, :] = near
                cells_b[span, :tail] = far
        return 0

    lax.fori_loop(0, used, forward, 0)
    load.wait()
    vloc_a[...] = vloc[:, :LANES]
    vloc_b[:, :tail] = vloc[:, LANES:]

    def strided(first, second, start, stride):
        span = pl.ds(start, half, stride=stride)
        return jnp.concatenate([first[span, :], second[span, :][:, :tail]], axis=1)

    def push(start, value):
        span = pl.ds(start, half, stride=2 * both)
        cells_a[span, :] = value[:, :LANES]
        cells_b[span, :] = jnp.concatenate([value[:, LANES:], jnp.zeros((half, LANES - tail), jnp.float32)], axis=1)

    def middle(k, _):
        def pull(start):
            return strided(cells_a, cells_b, start, 2 * both)

        re = jnp.concatenate([pull(k), pull(k + both)], axis=0).astype(jnp.bfloat16)
        im = jnp.concatenate([pull(k + rows), pull(k + rows + both)], axis=0).astype(jnp.bfloat16)
        cos, sin = along_z[0], along_z[1]
        zre = (dot(re, cos) - dot(im, sin)).astype(jnp.bfloat16)
        zim = (dot(re, sin) + dot(im, cos)).astype(jnp.bfloat16)
        even = dot(along_x[0], jnp.concatenate([zre[:half], zim[:half]], axis=0))
        odd = dot(along_x[1], jnp.concatenate([zre[half:], zim[half:]], axis=0))
        near = strided(vloc_a, vloc_b, k, planes)
        far = strided(vloc_a, vloc_b, k + half * planes, planes)
        first = (even + odd) * jnp.concatenate([near, near], axis=0)
        second = (even - odd) * jnp.concatenate([far, far], axis=0)
        even = dot(along_x[2], (first + second).astype(jnp.bfloat16)).astype(jnp.bfloat16)
        odd = dot(along_x[3], (first - second).astype(jnp.bfloat16)).astype(jnp.bfloat16)
        re = jnp.concatenate([even[:half], odd[:half]], axis=0)
        im = jnp.concatenate([even[half:], odd[half:]], axis=0)
        zre = dot(re, cos) + dot(im, sin)
        zim = dot(im, cos) - dot(re, sin)
        push(k, zre[:half])
        push(k + both, zre[half:])
        push(k + rows, zim[:half])
        push(k + rows + both, zim[half:])
        return 0

    lax.fori_loop(0, planes, middle, 0)

    def backward(c, _):
        for base in range(0, blocks, group):
            found = []
            for s in range(base, base + group):
                at = place(s, c)
                span = pl.ds(pl.multiple_of(at * both, 8), both)
                pick_z = where_bf16(level == row(s, 3, c), 1.0)
                part = jnp.concatenate([cells_a[span, :], cells_b[span, :tail]], axis=1)
                part = dot(part.astype(jnp.bfloat16), pick_z)
                phase = phases[s * chunks + c].astype(jnp.float32)
                re, im = part[:rows], part[rows:]
                cos, sin = phase[:rows], phase[rows:]
                found.append((jnp.sum(re * cos + im * sin, axis=0, keepdims=True),
                              jnp.sum(im * cos - re * sin, axis=0, keepdims=True)))
            for s, (re, im) in zip(range(base, base + group), found):
                result[pl.ds(s * 2 * chunks + c, 1), :] = re
                result[pl.ds((s * 2 + 1) * chunks + c, 1), :] = im
        return 0

    cells_a[spare * both :, :] = jnp.zeros((both, LANES), jnp.float32)
    cells_b[spare * both :, :] = jnp.zeros((both, LANES), jnp.float32)
    result[...] = jnp.zeros_like(result)
    lax.fori_loop(0, used, backward, 0)
    for s in range(blocks):
        outs[s][...] = result[s * 2 * chunks : (s + 1) * 2 * chunks, :].astype(jnp.bfloat16)


def lattice(pays, vloc, length, planes, chunks):
    blocks = len(pays)
    rows = round_up(planes, 8)
    own, along_z, along_x = tables_of(length, planes, blocks)
    vmem = pl.BlockSpec(memory_space=pltpu.VMEM)
    return pl.pallas_call(
        functools.partial(lattice_kernel, length, planes, chunks, blocks),
        out_shape=[jax.ShapeDtypeStruct((2 * chunks, LANES), jnp.bfloat16)] * blocks,
        in_specs=[vmem] * blocks + [pl.BlockSpec(memory_space=pl.ANY)] + [vmem] * 3,
        out_specs=[vmem] * blocks,
        scratch_shapes=[
            pltpu.VMEM((blocks * 4 * chunks, LANES), jnp.float32),
            pltpu.VMEM(((blocks * planes + 1) * 2 * rows, LANES), jnp.float32),
            pltpu.VMEM(((blocks * planes + 1) * 2 * rows, LANES), jnp.float32),
            pltpu.VMEM((blocks * chunks, 2 * rows, LANES), jnp.bfloat16),
            pltpu.VMEM((length * planes, length), jnp.float32),
            pltpu.VMEM((length * planes, LANES), jnp.float32),
            pltpu.VMEM((length * planes, LANES), jnp.float32),
            pltpu.VMEM((blocks * 2 * chunks, LANES), jnp.float32),
            pltpu.VMEM((blocks * 8, LANES), jnp.int32),
            pltpu.SMEM((blocks * 8, LANES), jnp.int32),
            pltpu.SemaphoreType.DMA((2,)),
        ],
        compiler_params=pltpu.CompilerParams(vmem_limit_bytes=VMEM_LIMIT),
        name="lattice",
    )(*pays, vloc.reshape(length * planes, length), own, along_z, along_x)


def finish_kernel(length, planes, chunks, blocks, *refs):
    parts = refs[:blocks]
    slot_ref, gvec_ref, psi_ref, extra_ref, out_ref = refs[blocks:]
    waves = slot_ref.shape[1]
    local = parts[0][...].astype(jnp.float32)
    for part in parts[1:]:
        local = local + part[...].astype(jnp.float32)
    turned = jnp.concatenate([local[:chunks].T, local[chunks:].T], axis=0).astype(jnp.bfloat16)
    x, y, z = cell_parts(gvec_ref[...], length)
    x = x + (lax.axis_index("pw") * planes).astype(jnp.float32)

    def fold(level):
        return jnp.where(level < length // 2, level, level - length)

    x, y, z = fold(x), fold(y), fold(z)
    kinetic = 4.0 * (x * x + y * y + z * z) / (length * length)
    slot = slot_ref[...]
    high = jnp.floor((slot + 0.5) * (1.0 / LANES))
    low = slot - high * LANES
    for tile in range(waves // LANES):
        span = slice(tile * LANES, (tile + 1) * LANES)
        at_high = where_bf16(iota((chunks, LANES), 0) == high[:, span], 1.0)
        rows = dot(turned, at_high)
        mine = iota((LANES, LANES), 0) == low[:, span]
        re = jnp.sum(jnp.where(mine, rows[:LANES], 0.0), axis=0, keepdims=True)
        im = jnp.sum(jnp.where(mine, rows[LANES:], 0.0), axis=0, keepdims=True)
        both = jnp.concatenate([re, im], axis=0)
        psi = psi_ref[:, span].astype(jnp.float32)
        out_ref[:, span] = (both + kinetic[:, span] * psi + extra_ref[:, span]).astype(jnp.bfloat16)


def finish(parts, slot, index, psi, extra, length, planes, chunks):
    blocks = len(parts)
    return pl.pallas_call(
        functools.partial(finish_kernel, length, planes, chunks, blocks),
        out_shape=jax.ShapeDtypeStruct(psi.shape, jnp.bfloat16),
        compiler_params=pltpu.CompilerParams(vmem_limit_bytes=VMEM_LIMIT),
        name="finish",
    )(*parts, slot, index, psi, extra)


def pair_dot(left, right):
    return jnp.einsum("bg,cg->bc", left, right, preferred_element_type=jnp.float32)


def swap(value, axis, step):
    size = lax.axis_size(axis)
    return lax.ppermute(value, axis, [(k, k ^ step) for k in range(size)])


def from_all(value, axis):
    size = lax.axis_size(axis)
    return [value] + [lax.ppermute(value, axis, [(k, (k + s) % size) for k in range(size)]) for s in range(1, size)]


def on_device(psi, gvec_index, vloc, beta, dmat, qmat):
    length = vloc.shape[0]
    planes = vloc.shape[1]
    width = psi.shape[2]
    blocks = lax.axis_size("pw")
    bands = lax.axis_size("band")
    chunks = round_up(width // LANES + planes, 16)
    waves = width * blocks
    atoms, each = dmat.shape[0], dmat.shape[1]
    index = gvec_index.reshape(1, width)
    mine = psi.reshape(2, width)
    pay, slot = group_waves(index, mine, length, planes, chunks)
    pays = [pay] + [swap(pay, "pw", s) for s in range(1, blocks)]
    every = jnp.stack(from_all(mine, "band"), axis=1)
    outs = lattice(pays, vloc, length, planes, chunks)
    parts = [outs[0]] + [swap(outs[s], "pw", s) for s in range(1, blocks)]

    proj_re = pair_dot(every[0], beta[0]) + pair_dot(every[1], beta[1])
    proj_im = pair_dot(every[1], beta[0]) - pair_dot(every[0], beta[1])
    over_re = pair_dot(every[0], mine[:1]) + pair_dot(every[1], mine[1:])
    over_im = pair_dot(every[1], mine[:1]) - pair_dot(every[0], mine[1:])
    partial = jnp.stack([jnp.concatenate([proj_re, over_re], 1), jnp.concatenate([proj_im, over_im], 1)])
    coef = functools.reduce(jnp.add, from_all(partial, "pw"))
    over = coef[:, :, -1]
    coef = coef[:, :, :-1]
    split = coef.reshape(2, bands, atoms, each)
    d_coef = jnp.einsum("aij,caj->cai", dmat, split[:, 0], precision=lax.Precision.HIGHEST)
    q_coef = jnp.einsum("aij,cbaj->cbai", qmat, split, precision=lax.Precision.HIGHEST)
    d_coef = d_coef.reshape(2, 1, atoms * each).astype(jnp.bfloat16)
    q_coef = q_coef.reshape(2, bands, atoms * each).astype(jnp.bfloat16)
    stacked = jnp.concatenate([d_coef, q_coef[:, :1]], axis=1)
    added_re = jnp.dot(stacked[0], beta[0], preferred_element_type=jnp.float32) - jnp.dot(stacked[1], beta[1], preferred_element_type=jnp.float32)
    added_im = jnp.dot(stacked[0], beta[1], preferred_element_type=jnp.float32) + jnp.dot(stacked[1], beta[0], preferred_element_type=jnp.float32)
    extra = jnp.stack([added_re[0], added_im[0]])
    spsi = mine.astype(jnp.float32) + jnp.stack([added_re[1], added_im[1]])
    spsi = spsi.astype(jnp.bfloat16).reshape(2, 1, width)
    wide = q_coef.astype(jnp.float32)
    own_re, own_im = coef[0, :1], coef[1, :1]
    gram_re = over[0] + jnp.sum(own_re * wide[0] + own_im * wide[1], axis=1)
    gram_im = over[1] + jnp.sum(own_re * wide[1] - own_im * wide[0], axis=1)
    gram = jnp.stack([gram_re, gram_im]) / waves
    order = (lax.axis_index("band") - jnp.arange(bands)) % bands
    gram = jnp.sum(jnp.where(order[None, :, None] == jnp.arange(bands)[None, None, :], gram[:, :, None], 0.0), axis=1)
    hpsi = finish(parts, slot, index, mine, extra, length, planes, chunks)
    return (hpsi.reshape(2, 1, width), spsi, gram.reshape(2, 1, bands))


def solution(mesh):
    in_specs = (P(None, "band", "pw"), P("pw"), P(None, "pw", None), P(None, None, "pw"), P(), P())
    out_specs = (P(None, "band", "pw"), P(None, "band", "pw"), P(None, "band", None))
    return jax.shard_map(
        on_device, mesh=mesh, in_specs=in_specs, out_specs=out_specs, check_vma=False
    )
```

```python
import functools

import jax
import jax.numpy as jnp
import ml_dtypes
import numpy as np
from jax import lax
from jax.experimental import pallas as pl
from jax.experimental.pallas import tpu as pltpu
from jax.sharding import PartitionSpec as P

LANES = 128
VMEM_LIMIT = 60 * 1024 * 1024


def round_up(value, unit):
    return -(-value // unit) * unit


def dft_parts(length):
    counter = np.arange(length)
    phase = counter[:, None] * counter[None, :] % length
    angle = phase.astype(np.float32) * np.float32(2.0 * np.pi / length)
    factor = np.float32(1.0) / np.sqrt(np.float32(length))
    return (np.cos(angle) * factor).astype(np.float32), (np.sin(angle) * factor).astype(np.float32)


def as_bf16(array):
    return np.asarray(array).astype(ml_dtypes.bfloat16)


def tables_of(length, planes, blocks):
    half = length // 2
    cosine, sine = dft_parts(length)
    rows = round_up(planes, 8)
    own = np.zeros((blocks, 2 * rows, length), np.float32)
    for block in range(blocks):
        span = slice(block * planes, (block + 1) * planes)
        own[block, :planes] = cosine[span]
        own[block, rows : rows + planes] = sine[span]
    def square(c, s, size):
        pad = ((0, size - half), (0, size - half))
        c, s = np.pad(c, pad), np.pad(s, pad)
        return np.block([[c, -s], [s, c]])

    first = slice(0, half)
    even, odd = slice(0, None, 2), slice(1, None, 2)
    along_z = np.stack(
        [
            square(cosine[even, first], -sine[even, first], LANES),
            square(cosine[odd, first], -sine[odd, first], LANES),
            square(cosine[first, even], sine[first, even], LANES),
            square(cosine[first, odd], sine[first, odd], LANES),
        ]
    )
    along_x = np.stack(
        [
            square(cosine[first, even], sine[first, even], half),
            square(cosine[first, odd], sine[first, odd], half),
            square(cosine[even, first], -sine[even, first], half),
            square(cosine[odd, first], -sine[odd, first], half),
        ]
    )
    return as_bf16(own), as_bf16(along_z), as_bf16(along_x)


def cell_parts(index, length):
    cell = index.astype(jnp.float32)
    x = jnp.floor((cell + 0.5) * (1.0 / (length * length)))
    rest = cell - x * (length * length)
    y = jnp.floor((rest + 0.5) * (1.0 / length))
    return x, y, rest - y * length


def iota(shape, dim):
    return lax.broadcasted_iota(jnp.int32, shape, dim).astype(jnp.float32)


def where_bf16(mask, value):
    return jnp.where(mask, value, 0.0).astype(jnp.bfloat16)


def dot(left, right):
    return jnp.dot(left, right, preferred_element_type=jnp.float32)


def dot_lanes(left, right):
    return lax.dot_general(left, right, (((1,), (1,)), ((), ())), preferred_element_type=jnp.float32)


def group_kernel(length, planes, chunks, gvec_ref, psi_ref, pay_ref, slot_ref, hot, counts, spread, pick):
    waves = gvec_ref.shape[1]
    tiles = waves // LANES
    rows = round_up(planes, 16)
    x, y, z = cell_parts(gvec_ref[...], length)
    z_half = jnp.floor(z * 0.5)
    z = z_half + (z - 2.0 * z_half) * LANES
    psi = psi_ref[...].astype(jnp.float32)
    plane = iota((rows, LANES), 0)
    for tile in range(tiles):
        span = slice(tile * LANES, (tile + 1) * LANES)
        hot[tile * rows : (tile + 1) * rows, :] = where_bf16(plane == x[:, span], 1.0)
    upto = jnp.where(iota((LANES, LANES), 0) <= iota((LANES, LANES), 1), 1.0, 0.0)
    upto = jnp.concatenate([upto, jnp.ones((LANES, LANES), jnp.float32)], axis=1)
    counts[...] = dot(hot[...], upto.astype(jnp.bfloat16))
    total = jnp.zeros((rows, LANES), jnp.float32)
    for tile in range(tiles):
        total = total + counts[tile * rows : (tile + 1) * rows, LANES:]
    need = jnp.maximum(jnp.floor((total + (LANES - 0.5)) * (1.0 / LANES)), 1.0)
    need = jnp.where(plane < planes, need, 0.0)
    below = where_bf16(iota((rows, rows), 1) < iota((rows, rows), 0), 1.0)
    first = dot(below, need.astype(jnp.bfloat16))
    ends = jnp.where((plane < planes) & (iota((rows, LANES), 1) >= first + need), 1.0, 0.0)
    chunk_plane = jnp.sum(ends, axis=0, keepdims=True)
    running = first * LANES - 1.0
    upper = iota((chunks, LANES), 0)
    lower = iota((LANES, LANES), 0)
    for tile in range(tiles):
        span = slice(tile * LANES, (tile + 1) * LANES)
        part = slice(tile * rows, (tile + 1) * rows)
        mine = plane == x[:, span]
        slot = jnp.where(mine, counts[part, :LANES] + running, 0.0)
        slot = jnp.sum(slot, axis=0, keepdims=True)
        running = running + counts[part, LANES:]
        slot_ref[:, span] = slot
        high = jnp.floor((slot + 0.5) * (1.0 / LANES))
        at_high = upper == high
        spread[0:chunks, span] = where_bf16(at_high, psi[0:1, span])
        spread[chunks : 2 * chunks, span] = where_bf16(at_high, psi[1:2, span])
        spread[2 * chunks : 3 * chunks, span] = where_bf16(at_high, y[:, span])
        spread[3 * chunks : 4 * chunks, span] = where_bf16(at_high, z[:, span])
        pick[:, span] = where_bf16(lower == slot - high * LANES, 1.0)
    pay_ref[0 : 4 * chunks, :] = dot_lanes(spread[...], pick[...]).astype(jnp.bfloat16)
    used = jnp.sum(need, axis=0, keepdims=True)
    pay_ref[4 * chunks :, :] = jnp.where(iota((16, LANES), 0) == 0.0, chunk_plane, used).astype(jnp.bfloat16)


def group_waves(index, psi, length, planes, chunks):
    waves = index.shape[1]
    rows = round_up(planes, 16)
    tiles = waves // LANES
    return pl.pallas_call(
        functools.partial(group_kernel, length, planes, chunks),
        out_shape=(
            jax.ShapeDtypeStruct((4 * chunks + 16, LANES), jnp.bfloat16),
            jax.ShapeDtypeStruct((1, waves), jnp.float32),
        ),
        scratch_shapes=[
            pltpu.VMEM((tiles * rows, LANES), jnp.bfloat16),
            pltpu.VMEM((tiles * rows, 2 * LANES), jnp.float32),
            pltpu.VMEM((4 * chunks, waves), jnp.bfloat16),
            pltpu.VMEM((LANES, waves), jnp.bfloat16),
        ],
        compiler_params=pltpu.CompilerParams(vmem_limit_bytes=VMEM_LIMIT),
        name="group_waves",
    )(index, psi)


def lattice_kernel(length, planes, chunks, blocks, *refs):
    pays = refs[:blocks]
    sums_ref, vloc_hbm, own_ref, along_z, along_x = refs[blocks : blocks + 5]
    outs = refs[blocks + 5 : 2 * blocks + 5]
    wide, cells_e, cells_o, phases, vloc, vloc_l, vloc_h, result, maps, maps_s, sems = refs[2 * blocks + 5 :]
    half = length // 2
    rows = round_up(planes, 8)
    both = 2 * rows
    pitch = both + 1
    spare = blocks * planes
    me = lax.axis_index("pw")
    load = pltpu.make_async_copy(vloc_hbm, vloc, sems.at[0])
    load.start()
    for s in range(blocks):
        maps[s * 8 : (s + 1) * 8, :] = pays[s][4 * chunks : 4 * chunks + 16, :].astype(jnp.int32)[:8]
    fetch = pltpu.make_async_copy(maps, maps_s, sems.at[1])
    fetch.start()
    for s in range(blocks):
        wide[s * 4 * chunks : (s + 1) * 4 * chunks, :] = pays[s][0 : 4 * chunks, :].astype(jnp.float32)
    own = own_ref[me]
    fetch.wait()
    used = maps_s[1, 0]
    for s in range(1, blocks):
        used = jnp.maximum(used, maps_s[s * 8 + 1, 0])
    level = iota((2 * LANES, LANES), 0)
    level_y = level[:length]
    group = 4 if blocks % 4 == 0 else 1
    ahead = 4 if blocks == group else 1
    batch = 4 if planes % 4 == 0 else 1
    turns = (used + ahead - 1) // ahead

    def place(s, c):
        at = maps_s[s * 8, c]
        x = (me ^ s) * planes + at
        return jnp.where(at < planes, x // 2 + x % 2 * half, spare)

    def row(s, part, c):
        return wide[pl.ds((s * 4 + part) * chunks + c, 1), :]

    def items(turn, base):
        return [(s, turn * ahead + j) for s in range(base, base + group) for j in range(ahead)]

    def pick_z(s, c):
        return where_bf16(level == row(s, 3, c), 1.0)

    def forward(turn, _):
        for base in range(0, blocks, group):
            todo = items(turn, base)
            found = [dot(own, where_bf16(level_y == row(s, 2, c), 1.0)) for s, c in todo]
            mixed = []
            for (s, c), phase in zip(todo, found):
                phases[s * chunks + c] = phase.astype(jnp.bfloat16)
                re, im = row(s, 0, c), row(s, 1, c)
                cos, sin = phase[:rows], phase[rows:]
                both_parts = jnp.concatenate([re * cos - im * sin, re * sin + im * cos], axis=0)
                mixed.append(both_parts.astype(jnp.bfloat16))
            found = [dot_lanes(value, pick_z(s, c)) for (s, c), value in zip(todo, mixed)]
            spans = [place(s, c) for s, c in todo]
            for n, (s, c) in enumerate(todo):
                span = pl.ds(spans[n] * pitch, both)
                if n % ahead == 0:
                    fresh = (c == 0) | (spans[n] != place(s, jnp.maximum(c - 1, 0)))
                    before_e, before_o = cells_e[span, :], cells_o[span, :]
                else:
                    fresh = spans[n] != spans[n - 1]
                    before_e, before_o = part_e, part_o
                part_e = found[n][:, :LANES] + jnp.where(fresh, 0.0, before_e)
                part_o = found[n][:, LANES:] + jnp.where(fresh, 0.0, before_o)
                cells_e[span, :] = part_e
                cells_o[span, :] = part_o
        return 0

    lax.fori_loop(0, turns, forward, 0)
    load.wait()
    step = planes + 1 - planes % 2

    def spread(x, _):
        plane = vloc[x]
        span = pl.ds(x * step, planes)
        vloc_l[span, :] = plane[:, :LANES]
        vloc_h[span, :] = jnp.concatenate([plane[:, half:], plane[:, : LANES - half]], axis=1)
        return 0

    lax.fori_loop(0, length, spread, 0, unroll=4)

    def strided(start):
        return pl.ds(start, half, stride=pitch)

    def beside(left, right):
        return jnp.concatenate([left, right], axis=1)

    def above(upper, lower):
        return jnp.concatenate([upper, lower], axis=0)

    def middle(turn, _):
        many = [turn * batch + j for j in range(batch)]
        starts = [k + odd * half * pitch for k in many for odd in range(2)]

        def pull(cells):
            return jnp.concatenate(
                [
                    beside(cells[strided(at), :], cells[strided(at + rows), :]).astype(jnp.bfloat16)
                    for at in starts
                ],
                axis=0,
            )

        even = dot(pull(cells_e), along_z[0])
        odd = dot(pull(cells_o), along_z[1])
        low, high = (even + odd).astype(jnp.bfloat16), (even - odd).astype(jnp.bfloat16)

        def stacked(n):
            part = slice(n * half, (n + 1) * half)
            return above(
                beside(low[part, :LANES], high[part, :LANES]),
                beside(low[part, LANES:], high[part, LANES:]),
            )

        sums, differences = [], []
        for j, k in enumerate(many):
            even = dot(along_x[0], stacked(2 * j))
            odd = dot(along_x[1], stacked(2 * j + 1))
            near, far = pl.ds(k, half, stride=step), pl.ds(k + half * step, half, stride=step)
            near = beside(vloc_l[near, :], vloc_h[near, :])
            far = beside(vloc_l[far, :], vloc_h[far, :])
            first = (even + odd) * above(near, near)
            second = (even - odd) * above(far, far)
            for table, value in ((along_x[2], first + second), (along_x[3], first - second)):
                back = dot(table, value.astype(jnp.bfloat16))
                total, change = back[:, :LANES] + back[:, LANES:], back[:, :LANES] - back[:, LANES:]
                sums.append(beside(total[:half], total[half:]).astype(jnp.bfloat16))
                differences.append(beside(change[:half], change[half:]).astype(jnp.bfloat16))
        even = dot(jnp.concatenate(sums, axis=0), along_z[2])
        odd = dot(jnp.concatenate(differences, axis=0), along_z[3])
        for n, at in enumerate(starts):
            part = slice(n * half, (n + 1) * half)
            cells_e[strided(at), :] = even[part, :LANES]
            cells_e[strided(at + rows), :] = even[part, LANES:]
            cells_o[strided(at), :] = odd[part, :LANES]
            cells_o[strided(at + rows), :] = odd[part, LANES:]
        return 0

    lax.fori_loop(0, planes // batch, middle, 0)

    def backward(turn, _):
        for base in range(0, blocks, group):
            todo = items(turn, base)
            found = []
            for s, c in todo:
                span = pl.ds(place(s, c) * pitch, both)
                value = beside(cells_e[span, :], cells_o[span, :]).astype(jnp.bfloat16)
                found.append(dot(value, pick_z(s, c)))
            for (s, c), part in zip(todo, found):
                phase = phases[s * chunks + c].astype(jnp.float32)
                re, im = part[:rows], part[rows:]
                cos, sin = phase[:rows], phase[rows:]
                result[pl.ds(s * 2 * chunks + c, 1), :] = jnp.sum(re * cos + im * sin, axis=0, keepdims=True)
                result[pl.ds((s * 2 + 1) * chunks + c, 1), :] = jnp.sum(im * cos - re * sin, axis=0, keepdims=True)
        return 0

    spare_span = pl.ds(spare * pitch, both)
    cells_e[spare_span, :] = jnp.zeros((both, LANES), jnp.float32)
    cells_o[spare_span, :] = jnp.zeros((both, LANES), jnp.float32)
    result[...] = jnp.zeros_like(result)
    lax.fori_loop(0, turns, backward, 0)
    rest = sums_ref[...]
    pieces = []
    for _ in range(3):
        pieces.append(rest.astype(jnp.bfloat16))
        rest = rest - pieces[-1].astype(jnp.float32)
    size = sums_ref.shape[0]
    for s in range(blocks):
        outs[s][0 : 2 * chunks, :] = result[s * 2 * chunks : (s + 1) * 2 * chunks, :].astype(jnp.bfloat16)
        for n, piece in enumerate(pieces):
            outs[s][2 * chunks + n * size : 2 * chunks + (n + 1) * size, :] = piece


def lattice(pays, sums, vloc, length, planes, chunks):
    blocks = len(pays)
    rows = round_up(planes, 8)
    own, along_z, along_x = tables_of(length, planes, blocks)
    vmem = pl.BlockSpec(memory_space=pltpu.VMEM)
    return pl.pallas_call(
        functools.partial(lattice_kernel, length, planes, chunks, blocks),
        out_shape=[jax.ShapeDtypeStruct((2 * chunks + 3 * sums.shape[0], LANES), jnp.bfloat16)] * blocks,
        in_specs=[vmem] * (blocks + 1) + [pl.BlockSpec(memory_space=pl.ANY)] + [vmem] * 3,
        out_specs=[vmem] * blocks,
        scratch_shapes=[
            pltpu.VMEM((blocks * 4 * chunks, LANES), jnp.float32),
            pltpu.VMEM((round_up((blocks * planes + 1) * (2 * rows + 1), 8), LANES), jnp.float32),
            pltpu.VMEM((round_up((blocks * planes + 1) * (2 * rows + 1), 8), LANES), jnp.float32),
            pltpu.VMEM((blocks * chunks, 2 * rows, LANES), jnp.bfloat16),
            pltpu.VMEM((length, planes, length), jnp.float32),
            pltpu.VMEM((round_up(length * (planes + 1), 8), LANES), jnp.float32),
            pltpu.VMEM((round_up(length * (planes + 1), 8), LANES), jnp.float32),
            pltpu.VMEM((blocks * 2 * chunks, LANES), jnp.float32),
            pltpu.VMEM((blocks * 8, LANES), jnp.int32),
            pltpu.SMEM((blocks * 8, LANES), jnp.int32),
            pltpu.SemaphoreType.DMA((2,)),
        ],
        compiler_params=pltpu.CompilerParams(vmem_limit_bytes=VMEM_LIMIT),
        name="lattice",
    )(*pays, sums, vloc, own, along_z, along_x)


def project_kernel(bands, *refs):
    every = [ref[...].astype(jnp.float32) for ref in refs[:bands]]
    beta_ref, out_ref = refs[bands:]
    count = beta_ref.shape[1]
    rows = out_ref.shape[0] // 2
    pad = [jnp.zeros_like(every[0][:1])] * (rows - bands)
    stack = [value[:1] for value in every] + pad + [value[1:] for value in every] + pad
    stack = jnp.concatenate(stack, axis=0).astype(jnp.bfloat16)

    def against(re, im):
        on_re, on_im = dot_lanes(stack, re), dot_lanes(stack, im)
        return jnp.concatenate([on_re[:rows] + on_im[rows:], on_re[rows:] - on_im[:rows]], axis=0)

    out_ref[...] = jnp.zeros_like(out_ref)
    out_ref[:, :count] = against(beta_ref[0], beta_ref[1])
    shape = (16, every[0].shape[1])
    own = [jnp.broadcast_to(every[0][n : n + 1], shape).astype(jnp.bfloat16) for n in range(2)]
    over = against(*own)[:, :1]
    out_ref[...] = jnp.where(iota(out_ref.shape, 1) == count, over, out_ref[...])


def project(every, beta):
    bands = len(every)
    return pl.pallas_call(
        functools.partial(project_kernel, bands),
        out_shape=jax.ShapeDtypeStruct((2 * round_up(bands, 8), LANES), jnp.float32),
        compiler_params=pltpu.CompilerParams(vmem_limit_bytes=VMEM_LIMIT),
        name="project",
    )(*every, beta)


def finish_kernel(length, planes, chunks, blocks, bands, *refs):
    parts = refs[:blocks]
    slot_ref, gvec_ref, psi_ref, beta_ref, atoms_ref, hpsi_ref, spsi_ref, gram_ref = refs[blocks:]
    waves = slot_ref.shape[1]
    count = beta_ref.shape[1]
    total = parts[0][...].astype(jnp.float32)
    for part in parts[1:]:
        total = total + part[...].astype(jnp.float32)
    size = (total.shape[0] - 2 * chunks) // 3
    half_size = size // 2
    sums = [total[2 * chunks + n * size : 2 * chunks + (n + 1) * size] for n in range(3)]
    sums = sums[0] + (sums[1] + sums[2])
    coef = jnp.dot(sums, atoms_ref[...], precision=lax.Precision.HIGHEST, preferred_element_type=jnp.float32)
    coef = coef.astype(jnp.bfloat16).astype(jnp.float32)
    d_re, d_im = coef[:1, :count], coef[half_size : half_size + 1, :count]
    q_re, q_im = coef[:1, LANES : LANES + count], coef[half_size : half_size + 1, LANES : LANES + count]
    none = jnp.zeros((4, count), jnp.float32)
    on_re = jnp.concatenate([d_re, d_im, q_re, q_im, none], axis=0).astype(jnp.bfloat16)
    on_im = jnp.concatenate([-d_im, d_re, -q_im, q_re, none], axis=0).astype(jnp.bfloat16)
    added = dot(on_re, beta_ref[0]) + dot(on_im, beta_ref[1])

    own_re, own_im = sums[:1], sums[half_size : half_size + 1]
    each_re, each_im = coef[:half_size, LANES:], coef[half_size:, LANES:]
    over = iota((half_size, LANES), 1) == count
    gram_re = own_re * each_re + own_im * each_im + jnp.where(over, sums[:half_size], 0.0)
    gram_im = own_re * each_im - own_im * each_re + jnp.where(over, sums[half_size:], 0.0)
    turn = lax.axis_index("band") - lax.broadcasted_iota(jnp.int32, (half_size, bands), 0)
    turn = jnp.where(turn < 0, turn + bands, turn)
    here = turn == lax.broadcasted_iota(jnp.int32, (half_size, bands), 1)
    here = here & (lax.broadcasted_iota(jnp.int32, (half_size, bands), 0) < bands)
    for n, value in enumerate((gram_re, gram_im)):
        value = jnp.sum(value, axis=1, keepdims=True)
        value = jnp.sum(jnp.where(here, value, 0.0), axis=0, keepdims=True)
        gram_ref[n : n + 1, :] = value * (1.0 / (waves * blocks))

    local = total[: 2 * chunks]
    turned = jnp.concatenate([local[:chunks].T, local[chunks:].T], axis=0).astype(jnp.bfloat16)
    x, y, z = cell_parts(gvec_ref[...], length)
    x = x + (lax.axis_index("pw") * planes).astype(jnp.float32)

    def fold(level):
        return jnp.where(level < length // 2, level, level - length)

    x, y, z = fold(x), fold(y), fold(z)
    kinetic = 4.0 * (x * x + y * y + z * z) / (length * length)
    slot = slot_ref[...]
    high = jnp.floor((slot + 0.5) * (1.0 / LANES))
    low = slot - high * LANES
    for tile in range(waves // LANES):
        span = slice(tile * LANES, (tile + 1) * LANES)
        at_high = where_bf16(iota((chunks, LANES), 0) == high[:, span], 1.0)
        rows = dot(turned, at_high)
        mine = iota((LANES, LANES), 0) == low[:, span]
        re = jnp.sum(jnp.where(mine, rows[:LANES], 0.0), axis=0, keepdims=True)
        im = jnp.sum(jnp.where(mine, rows[LANES:], 0.0), axis=0, keepdims=True)
        both = jnp.concatenate([re, im], axis=0)
        psi = psi_ref[:, span].astype(jnp.float32)
        hpsi_ref[:, span] = (both + kinetic[:, span] * psi + added[0:2, span]).astype(jnp.bfloat16)
        spsi_ref[:, span] = (psi + added[2:4, span]).astype(jnp.bfloat16)


def finish(parts, slot, index, psi, beta, atoms, length, planes, chunks, bands):
    blocks = len(parts)
    return pl.pallas_call(
        functools.partial(finish_kernel, length, planes, chunks, blocks, bands),
        out_shape=(
            jax.ShapeDtypeStruct(psi.shape, jnp.bfloat16),
            jax.ShapeDtypeStruct(psi.shape, jnp.bfloat16),
            jax.ShapeDtypeStruct((2, bands), jnp.float32),
        ),
        compiler_params=pltpu.CompilerParams(vmem_limit_bytes=VMEM_LIMIT),
        name="finish",
    )(*parts, slot, index, psi, beta, atoms)


def swap(value, axis, step):
    size = lax.axis_size(axis)
    return lax.ppermute(value, axis, [(k, k ^ step) for k in range(size)])


def from_all(value, axis):
    size = lax.axis_size(axis)
    return [value] + [lax.ppermute(value, axis, [(k, (k + s) % size) for k in range(size)]) for s in range(1, size)]


def atom_blocks(matrix):
    atoms, each = matrix.shape[0], matrix.shape[1]
    same = jnp.eye(atoms, dtype=matrix.dtype)[:, None, :, None]
    square = (same * jnp.transpose(matrix, (0, 2, 1))[:, :, None, :]).reshape(atoms * each, atoms * each)
    return jnp.pad(square, ((0, LANES - atoms * each), (0, LANES - atoms * each)))


def on_device(psi, gvec_index, vloc, beta, dmat, qmat):
    length = vloc.shape[0]
    planes = vloc.shape[1]
    width = psi.shape[2]
    blocks = lax.axis_size("pw")
    bands = lax.axis_size("band")
    chunks = round_up(width // LANES + planes, 16)
    index = gvec_index.reshape(1, width)
    mine = psi.reshape(2, width)
    atoms = jnp.concatenate([atom_blocks(dmat), atom_blocks(qmat)], axis=1)
    pay, slot = group_waves(index, mine, length, planes, chunks)
    pays = [pay] + [swap(pay, "pw", s) for s in range(1, blocks)]
    later, _ = lax.optimization_barrier((mine, pay))
    sums = project(from_all(later, "band"), beta)
    outs = lattice(pays, sums, vloc, length, planes, chunks)
    parts = [outs[0]] + [swap(outs[s], "pw", s) for s in range(1, blocks)]
    hpsi, spsi, gram = finish(parts, slot, index, mine, beta, atoms, length, planes, chunks, bands)
    return (hpsi.reshape(2, 1, width), spsi.reshape(2, 1, width), gram.reshape(2, 1, bands))


def solution(mesh):
    in_specs = (P(None, "band", "pw"), P("pw"), P(None, "pw", None), P(None, None, "pw"), P(), P())
    out_specs = (P(None, "band", "pw"), P(None, "band", "pw"), P(None, "band", None))
    return jax.shard_map(
        on_device, mesh=mesh, in_specs=in_specs, out_specs=out_specs, check_vma=False
    )
```

```python
import functools

import jax
import jax.numpy as jnp
import ml_dtypes
import numpy as np
from jax import lax
from jax.experimental import pallas as pl
from jax.experimental.pallas import tpu as pltpu
from jax.sharding import PartitionSpec as P

LANES = 128
VMEM_LIMIT = 60 * 1024 * 1024


def round_up(value, unit):
    return -(-value // unit) * unit


def dft_parts(length):
    counter = np.arange(length)
    phase = counter[:, None] * counter[None, :] % length
    angle = phase.astype(np.float32) * np.float32(2.0 * np.pi / length)
    factor = np.float32(1.0) / np.sqrt(np.float32(length))
    return (np.cos(angle) * factor).astype(np.float32), (np.sin(angle) * factor).astype(np.float32)


def as_bf16(array):
    return np.asarray(array).astype(ml_dtypes.bfloat16)


def tables_of(length, planes, blocks):
    half = length // 2
    cosine, sine = dft_parts(length)
    rows = round_up(planes, 8)
    own = np.zeros((blocks, 2 * rows, length), np.float32)
    for block in range(blocks):
        span = slice(block * planes, (block + 1) * planes)
        own[block, :planes] = cosine[span]
        own[block, rows : rows + planes] = sine[span]
    def square(c, s, size):
        pad = ((0, size - half), (0, size - half))
        c, s = np.pad(c, pad), np.pad(s, pad)
        return np.block([[c, -s], [s, c]])

    first = slice(0, half)
    even, odd = slice(0, None, 2), slice(1, None, 2)
    along_z = np.stack(
        [
            square(cosine[even, first], -sine[even, first], LANES),
            square(cosine[odd, first], -sine[odd, first], LANES),
            square(cosine[first, even], sine[first, even], LANES),
            square(cosine[first, odd], sine[first, odd], LANES),
        ]
    )
    along_x = np.stack(
        [
            square(cosine[first, even], sine[first, even], half),
            square(cosine[first, odd], sine[first, odd], half),
            square(cosine[even, first], -sine[even, first], half),
            square(cosine[odd, first], -sine[odd, first], half),
        ]
    )
    return as_bf16(own), as_bf16(along_z), as_bf16(along_x)


def cell_parts(index, length):
    cell = index.astype(jnp.float32)
    x = jnp.floor((cell + 0.5) * (1.0 / (length * length)))
    rest = cell - x * (length * length)
    y = jnp.floor((rest + 0.5) * (1.0 / length))
    return x, y, rest - y * length


def iota(shape, dim):
    return lax.broadcasted_iota(jnp.int32, shape, dim).astype(jnp.float32)


def where_bf16(mask, value):
    return jnp.where(mask, value, 0.0).astype(jnp.bfloat16)


def dot(left, right):
    return jnp.dot(left, right, preferred_element_type=jnp.float32)


def dot_lanes(left, right):
    return lax.dot_general(left, right, (((1,), (1,)), ((), ())), preferred_element_type=jnp.float32)


def group_kernel(length, planes, chunks, gvec_ref, psi_ref, pay_ref, slot_ref, hot, counts, spread, pick):
    waves = gvec_ref.shape[1]
    tiles = waves // LANES
    rows = round_up(planes, 16)
    x, y, z = cell_parts(gvec_ref[...], length)
    z_half = jnp.floor(z * 0.5)
    z = z_half + (z - 2.0 * z_half) * LANES
    psi = psi_ref[...].astype(jnp.float32)
    plane = iota((rows, LANES), 0)
    for tile in range(tiles):
        span = slice(tile * LANES, (tile + 1) * LANES)
        hot[tile * rows : (tile + 1) * rows, :] = where_bf16(plane == x[:, span], 1.0)
    upto = jnp.where(iota((LANES, LANES), 0) <= iota((LANES, LANES), 1), 1.0, 0.0)
    upto = jnp.concatenate([upto, jnp.ones((LANES, LANES), jnp.float32)], axis=1)
    counts[...] = dot(hot[...], upto.astype(jnp.bfloat16))
    total = jnp.zeros((rows, LANES), jnp.float32)
    for tile in range(tiles):
        total = total + counts[tile * rows : (tile + 1) * rows, LANES:]
    need = jnp.maximum(jnp.floor((total + (LANES - 0.5)) * (1.0 / LANES)), 1.0)
    need = jnp.where(plane < planes, need, 0.0)
    below = where_bf16(iota((rows, rows), 1) < iota((rows, rows), 0), 1.0)
    first = dot(below, need.astype(jnp.bfloat16))
    ends = jnp.where((plane < planes) & (iota((rows, LANES), 1) >= first + need), 1.0, 0.0)
    chunk_plane = jnp.sum(ends, axis=0, keepdims=True)
    running = first * LANES - 1.0
    upper = iota((chunks, LANES), 0)
    lower = iota((LANES, LANES), 0)
    for tile in range(tiles):
        span = slice(tile * LANES, (tile + 1) * LANES)
        part = slice(tile * rows, (tile + 1) * rows)
        mine = plane == x[:, span]
        slot = jnp.where(mine, counts[part, :LANES] + running, 0.0)
        slot = jnp.sum(slot, axis=0, keepdims=True)
        running = running + counts[part, LANES:]
        slot_ref[:, span] = slot
        high = jnp.floor((slot + 0.5) * (1.0 / LANES))
        at_high = upper == high
        spread[0:chunks, span] = where_bf16(at_high, psi[0:1, span])
        spread[chunks : 2 * chunks, span] = where_bf16(at_high, psi[1:2, span])
        spread[2 * chunks : 3 * chunks, span] = where_bf16(at_high, y[:, span])
        spread[3 * chunks : 4 * chunks, span] = where_bf16(at_high, z[:, span])
        pick[:, span] = where_bf16(lower == slot - high * LANES, 1.0)
    pay_ref[0 : 4 * chunks, :] = dot_lanes(spread[...], pick[...]).astype(jnp.bfloat16)
    used = jnp.sum(need, axis=0, keepdims=True)
    pay_ref[4 * chunks :, :] = jnp.where(iota((16, LANES), 0) == 0.0, chunk_plane, used).astype(jnp.bfloat16)


def group_waves(index, psi, length, planes, chunks):
    waves = index.shape[1]
    rows = round_up(planes, 16)
    tiles = waves // LANES
    return pl.pallas_call(
        functools.partial(group_kernel, length, planes, chunks),
        out_shape=(
            jax.ShapeDtypeStruct((4 * chunks + 16, LANES), jnp.bfloat16),
            jax.ShapeDtypeStruct((1, waves), jnp.float32),
        ),
        scratch_shapes=[
            pltpu.VMEM((tiles * rows, LANES), jnp.bfloat16),
            pltpu.VMEM((tiles * rows, 2 * LANES), jnp.float32),
            pltpu.VMEM((4 * chunks, waves), jnp.bfloat16),
            pltpu.VMEM((LANES, waves), jnp.bfloat16),
        ],
        compiler_params=pltpu.CompilerParams(vmem_limit_bytes=VMEM_LIMIT),
        name="group_waves",
    )(index, psi)


def lattice_kernel(length, planes, chunks, blocks, *refs):
    pays = refs[:blocks]
    sums_ref, vloc_hbm, own_ref, along_z, along_x = refs[blocks : blocks + 5]
    outs = refs[blocks + 5 : 2 * blocks + 5]
    wide, cells_e, cells_o, phases, vloc, result, maps, maps_s, sems = refs[2 * blocks + 5 :]
    half = length // 2
    rows = round_up(planes, 8)
    both = 2 * rows
    pitch = both + 1
    spare = blocks * planes
    me = lax.axis_index("pw")

    def load(k, _):
        pltpu.make_async_copy(vloc_hbm.at[:, k, :], vloc.at[k], sems.at[0]).start()
        return 0

    lax.fori_loop(0, planes, load, 0)
    for s in range(blocks):
        maps[s * 8 : (s + 1) * 8, :] = pays[s][4 * chunks : 4 * chunks + 16, :].astype(jnp.int32)[:8]
    fetch = pltpu.make_async_copy(maps, maps_s, sems.at[1])
    fetch.start()
    for s in range(blocks):
        wide[s * 4 * chunks : (s + 1) * 4 * chunks, :] = pays[s][0 : 4 * chunks, :].astype(jnp.float32)
    own = own_ref[me]
    fetch.wait()
    used = maps_s[1, 0]
    for s in range(1, blocks):
        used = jnp.maximum(used, maps_s[s * 8 + 1, 0])
    level = iota((2 * LANES, LANES), 0)
    level_y = level[:length]
    group = 4 if blocks % 4 == 0 else 1
    ahead = 8 if blocks == group else 1
    batch = 8 if planes % 8 == 0 else 1
    turns = (used + ahead - 1) // ahead

    def place(s, c):
        at = maps_s[s * 8, c]
        x = (me ^ s) * planes + at
        return jnp.where(at < planes, x // 2 + x % 2 * half, spare)

    def row(s, part, c):
        return wide[pl.ds((s * 4 + part) * chunks + c, 1), :]

    def items(turn, base):
        return [(s, turn * ahead + j) for s in range(base, base + group) for j in range(ahead)]

    def pick_z(s, c):
        return where_bf16(level == row(s, 3, c), 1.0)

    def phases_of(todo):
        wanted = [where_bf16(level_y == row(s, 2, c), 1.0) for s, c in todo]
        found = []
        for n in range(0, len(todo), 2):
            both_phases = dot(own, jnp.concatenate(wanted[n : n + 2], axis=1))
            found += [both_phases[:, :LANES], both_phases[:, LANES:]][: len(wanted[n : n + 2])]
        return found

    def forward(turn, _):
        for base in range(0, blocks, group):
            todo = items(turn, base)
            found = phases_of(todo)
            mixed = []
            for (s, c), phase in zip(todo, found):
                phases[s * chunks + c] = phase.astype(jnp.bfloat16)
                re, im = row(s, 0, c), row(s, 1, c)
                cos, sin = phase[:rows], phase[rows:]
                both_parts = jnp.concatenate([re * cos - im * sin, re * sin + im * cos], axis=0)
                mixed.append(both_parts.astype(jnp.bfloat16))
            found = [dot_lanes(value, pick_z(s, c)) for (s, c), value in zip(todo, mixed)]
            spans = [place(s, c) for s, c in todo]
            for n, (s, c) in enumerate(todo):
                span = pl.ds(spans[n] * pitch, both)
                if n % ahead == 0:
                    fresh = (c == 0) | (spans[n] != place(s, jnp.maximum(c - 1, 0)))
                    before_e, before_o = cells_e[span, :], cells_o[span, :]
                else:
                    fresh = spans[n] != spans[n - 1]
                    before_e, before_o = part_e, part_o
                part_e = found[n][:, :LANES] + jnp.where(fresh, 0.0, before_e)
                part_o = found[n][:, LANES:] + jnp.where(fresh, 0.0, before_o)
                cells_e[span, :] = part_e
                cells_o[span, :] = part_o
        return 0

    lax.fori_loop(0, turns, forward, 0)
    pltpu.make_async_copy(vloc, vloc, sems.at[0]).wait()

    def strided(start):
        return pl.ds(start, half, stride=pitch)

    def beside(left, right):
        return jnp.concatenate([left, right], axis=1)

    def above(upper, lower):
        return jnp.concatenate([upper, lower], axis=0)

    def middle(turn, _):
        many = [turn * batch + j for j in range(batch)]
        starts = [k + odd * half * pitch for k in many for odd in range(2)]

        def pull(cells):
            return jnp.concatenate(
                [
                    beside(cells[strided(at), :], cells[strided(at + rows), :]).astype(jnp.bfloat16)
                    for at in starts
                ],
                axis=0,
            )

        even = dot(pull(cells_e), along_z[0])
        odd = dot(pull(cells_o), along_z[1])
        low, high = (even + odd).astype(jnp.bfloat16), (even - odd).astype(jnp.bfloat16)

        def stacked(n):
            part = slice(n * half, (n + 1) * half)
            return above(
                beside(low[part, :LANES], high[part, :LANES]),
                beside(low[part, LANES:], high[part, LANES:]),
            )

        sums, differences = [], []
        for j, k in enumerate(many):
            even = dot(along_x[0], stacked(2 * j))
            odd = dot(along_x[1], stacked(2 * j + 1))
            field = vloc[k]
            field = beside(field[:, :LANES], beside(field[:, half:], field[:, : LANES - half]))
            near, far = field[:half], field[half:]
            first = (even + odd) * above(near, near)
            second = (even - odd) * above(far, far)
            for table, value in ((along_x[2], first + second), (along_x[3], first - second)):
                back = dot(table, value.astype(jnp.bfloat16))
                total, change = back[:, :LANES] + back[:, LANES:], back[:, :LANES] - back[:, LANES:]
                sums.append(beside(total[:half], total[half:]).astype(jnp.bfloat16))
                differences.append(beside(change[:half], change[half:]).astype(jnp.bfloat16))
        even = dot(jnp.concatenate(sums, axis=0), along_z[2])
        odd = dot(jnp.concatenate(differences, axis=0), along_z[3])
        for n, at in enumerate(starts):
            part = slice(n * half, (n + 1) * half)
            cells_e[strided(at), :] = even[part, :LANES]
            cells_e[strided(at + rows), :] = even[part, LANES:]
            cells_o[strided(at), :] = odd[part, :LANES]
            cells_o[strided(at + rows), :] = odd[part, LANES:]
        return 0

    lax.fori_loop(0, planes // batch, middle, 0)

    def backward(turn, _):
        for base in range(0, blocks, group):
            todo = items(turn, base)
            found = []
            for s, c in todo:
                span = pl.ds(place(s, c) * pitch, both)
                value = beside(cells_e[span, :], cells_o[span, :]).astype(jnp.bfloat16)
                found.append(dot(value, pick_z(s, c)))
            for (s, c), part in zip(todo, found):
                phase = phases[s * chunks + c].astype(jnp.float32)
                re, im = part[:rows], part[rows:]
                cos, sin = phase[:rows], phase[rows:]
                result[pl.ds(s * 2 * chunks + c, 1), :] = jnp.sum(re * cos + im * sin, axis=0, keepdims=True)
                result[pl.ds((s * 2 + 1) * chunks + c, 1), :] = jnp.sum(im * cos - re * sin, axis=0, keepdims=True)
        return 0

    spare_span = pl.ds(spare * pitch, both)
    cells_e[spare_span, :] = jnp.zeros((both, LANES), jnp.float32)
    cells_o[spare_span, :] = jnp.zeros((both, LANES), jnp.float32)
    result[...] = jnp.zeros_like(result)
    lax.fori_loop(0, turns, backward, 0)
    rest = sums_ref[...]
    pieces = []
    for _ in range(3):
        pieces.append(rest.astype(jnp.bfloat16))
        rest = rest - pieces[-1].astype(jnp.float32)
    size = sums_ref.shape[0]
    for s in range(blocks):
        outs[s][0 : 2 * chunks, :] = result[s * 2 * chunks : (s + 1) * 2 * chunks, :].astype(jnp.bfloat16)
        for n, piece in enumerate(pieces):
            outs[s][2 * chunks + n * size : 2 * chunks + (n + 1) * size, :] = piece


def lattice(pays, sums, vloc, length, planes, chunks):
    blocks = len(pays)
    rows = round_up(planes, 8)
    own, along_z, along_x = tables_of(length, planes, blocks)
    vmem = pl.BlockSpec(memory_space=pltpu.VMEM)
    return pl.pallas_call(
        functools.partial(lattice_kernel, length, planes, chunks, blocks),
        out_shape=[jax.ShapeDtypeStruct((2 * chunks + 3 * sums.shape[0], LANES), jnp.bfloat16)] * blocks,
        in_specs=[vmem] * (blocks + 1) + [pl.BlockSpec(memory_space=pl.ANY)] + [vmem] * 3,
        out_specs=[vmem] * blocks,
        scratch_shapes=[
            pltpu.VMEM((blocks * 4 * chunks, LANES), jnp.float32),
            pltpu.VMEM((round_up((blocks * planes + 1) * (2 * rows + 1), 8), LANES), jnp.float32),
            pltpu.VMEM((round_up((blocks * planes + 1) * (2 * rows + 1), 8), LANES), jnp.float32),
            pltpu.VMEM((blocks * chunks, 2 * rows, LANES), jnp.bfloat16),
            pltpu.VMEM((planes, length, length), jnp.float32),
            pltpu.VMEM((blocks * 2 * chunks, LANES), jnp.float32),
            pltpu.VMEM((blocks * 8, LANES), jnp.int32),
            pltpu.SMEM((blocks * 8, LANES), jnp.int32),
            pltpu.SemaphoreType.DMA((2,)),
        ],
        compiler_params=pltpu.CompilerParams(vmem_limit_bytes=VMEM_LIMIT),
        name="lattice",
    )(*pays, sums, vloc, own, along_z, along_x)


def project_kernel(bands, *refs):
    every = [ref[...].astype(jnp.float32) for ref in refs[:-2]]
    beta_ref, out_ref = refs[-2:]
    count = beta_ref.shape[0] // 2
    rows = out_ref.shape[0] // 2
    pad = [jnp.zeros((rows - bands, every[0].shape[2]), jnp.float32)] if rows > bands else []
    re = jnp.concatenate([value[0] for value in every] + pad, axis=0)
    im = jnp.concatenate([value[1] for value in every] + pad, axis=0)
    found = dot_lanes(beta_ref[...], jnp.concatenate([re, im], axis=0).astype(jnp.bfloat16))
    on_re, on_im = found[:count], found[count:]
    found = jnp.concatenate([on_re[:, :rows] + on_im[:, rows:], on_re[:, rows:] - on_im[:, :rows]], axis=1)
    out_ref[...] = jnp.zeros_like(out_ref)
    out_ref[:, :count] = found.T
    own_re, own_im = re[:1], im[:1]
    over = jnp.concatenate(
        [
            jnp.sum(re * own_re + im * own_im, axis=1, keepdims=True),
            jnp.sum(im * own_re - re * own_im, axis=1, keepdims=True),
        ],
        axis=0,
    )
    out_ref[...] = jnp.where(iota(out_ref.shape, 1) == count, over, out_ref[...])


def project(every, beta, bands):
    return pl.pallas_call(
        functools.partial(project_kernel, bands),
        out_shape=jax.ShapeDtypeStruct((2 * round_up(bands, 8), LANES), jnp.float32),
        compiler_params=pltpu.CompilerParams(vmem_limit_bytes=VMEM_LIMIT),
        name="project",
    )(*every, beta.reshape(2 * beta.shape[1], beta.shape[2]))


def finish_kernel(length, planes, chunks, blocks, bands, *refs):
    parts = refs[:blocks]
    slot_ref, gvec_ref, psi_ref, beta_ref, atoms_ref, hpsi_ref, spsi_ref, gram_ref = refs[blocks:]
    waves = slot_ref.shape[1]
    count = beta_ref.shape[1]
    total = parts[0][...].astype(jnp.float32)
    for part in parts[1:]:
        total = total + part[...].astype(jnp.float32)
    size = (total.shape[0] - 2 * chunks) // 3
    half_size = size // 2
    sums = [total[2 * chunks + n * size : 2 * chunks + (n + 1) * size] for n in range(3)]
    sums = sums[0] + (sums[1] + sums[2])
    coef = jnp.dot(sums, atoms_ref[...], precision=lax.Precision.HIGHEST, preferred_element_type=jnp.float32)
    coef = coef.astype(jnp.bfloat16).astype(jnp.float32)
    d_re, d_im = coef[:1, :count], coef[half_size : half_size + 1, :count]
    q_re, q_im = coef[:1, LANES : LANES + count], coef[half_size : half_size + 1, LANES : LANES + count]
    none = jnp.zeros((4, count), jnp.float32)
    on_re = jnp.concatenate([d_re, d_im, q_re, q_im, none], axis=0).astype(jnp.bfloat16)
    on_im = jnp.concatenate([-d_im, d_re, -q_im, q_re, none], axis=0).astype(jnp.bfloat16)
    added = dot(on_re, beta_ref[0]) + dot(on_im, beta_ref[1])

    own_re, own_im = sums[:1], sums[half_size : half_size + 1]
    each_re, each_im = coef[:half_size, LANES:], coef[half_size:, LANES:]
    over = iota((half_size, LANES), 1) == count
    gram_re = own_re * each_re + own_im * each_im + jnp.where(over, sums[:half_size], 0.0)
    gram_im = own_re * each_im - own_im * each_re + jnp.where(over, sums[half_size:], 0.0)
    slot_at = lax.broadcasted_iota(jnp.int32, (half_size, bands), 0)
    if doubles(bands):
        turn = lax.axis_index("band") ^ slot_at
    else:
        turn = lax.axis_index("band") - slot_at
        turn = jnp.where(turn < 0, turn + bands, turn)
    here = turn == lax.broadcasted_iota(jnp.int32, (half_size, bands), 1)
    here = here & (lax.broadcasted_iota(jnp.int32, (half_size, bands), 0) < bands)
    for n, value in enumerate((gram_re, gram_im)):
        value = jnp.sum(value, axis=1, keepdims=True)
        value = jnp.sum(jnp.where(here, value, 0.0), axis=0, keepdims=True)
        gram_ref[n : n + 1, :] = value * (1.0 / (waves * blocks))

    local = total[: 2 * chunks]
    turned = jnp.concatenate([local[:chunks].T, local[chunks:].T], axis=0).astype(jnp.bfloat16)
    x, y, z = cell_parts(gvec_ref[...], length)
    x = x + (lax.axis_index("pw") * planes).astype(jnp.float32)

    def fold(level):
        return jnp.where(level < length // 2, level, level - length)

    x, y, z = fold(x), fold(y), fold(z)
    kinetic = 4.0 * (x * x + y * y + z * z) / (length * length)
    slot = slot_ref[...]
    high = jnp.floor((slot + 0.5) * (1.0 / LANES))
    low = slot - high * LANES
    for tile in range(waves // LANES):
        span = slice(tile * LANES, (tile + 1) * LANES)
        at_high = where_bf16(iota((chunks, LANES), 0) == high[:, span], 1.0)
        rows = dot(turned, at_high)
        mine = iota((LANES, LANES), 0) == low[:, span]
        re = jnp.sum(jnp.where(mine, rows[:LANES], 0.0), axis=0, keepdims=True)
        im = jnp.sum(jnp.where(mine, rows[LANES:], 0.0), axis=0, keepdims=True)
        both = jnp.concatenate([re, im], axis=0)
        psi = psi_ref[:, span].astype(jnp.float32)
        hpsi_ref[:, span] = (both + kinetic[:, span] * psi + added[0:2, span]).astype(jnp.bfloat16)
        spsi_ref[:, span] = (psi + added[2:4, span]).astype(jnp.bfloat16)


def finish(parts, slot, index, psi, beta, atoms, length, planes, chunks, bands):
    blocks = len(parts)
    return pl.pallas_call(
        functools.partial(finish_kernel, length, planes, chunks, blocks, bands),
        out_shape=(
            jax.ShapeDtypeStruct(psi.shape, jnp.bfloat16),
            jax.ShapeDtypeStruct(psi.shape, jnp.bfloat16),
            jax.ShapeDtypeStruct((2, bands), jnp.float32),
        ),
        compiler_params=pltpu.CompilerParams(vmem_limit_bytes=VMEM_LIMIT),
        name="finish",
    )(*parts, slot, index, psi, beta, atoms)


def swap(value, axis, step):
    size = lax.axis_size(axis)
    return lax.ppermute(value, axis, [(k, k ^ step) for k in range(size)])


def doubles(size):
    return size & (size - 1) == 0


def from_blocks(value, axis):
    size = lax.axis_size(axis)
    found = {0: value}
    step = size // 2
    while step:
        found.update({s + step: swap(found[s], axis, step) for s in list(found)})
        step //= 2
    return [found[s] for s in range(size)]


def from_bands(value, axis):
    size = lax.axis_size(axis)
    if not doubles(size):
        pairs = [[(k, (k + s) % size) for k in range(size)] for s in range(1, size)]
        return [value] + [lax.ppermute(value, axis, pair) for pair in pairs]
    held = [value]
    step = 1
    while step < size:
        value = jnp.concatenate(held, axis=1)
        held = [value, swap(value, axis, step)]
        step *= 2
    return held


def atom_blocks(matrix):
    atoms, each = matrix.shape[0], matrix.shape[1]
    same = jnp.eye(atoms, dtype=matrix.dtype)[:, None, :, None]
    square = (same * jnp.transpose(matrix, (0, 2, 1))[:, :, None, :]).reshape(atoms * each, atoms * each)
    return jnp.pad(square, ((0, LANES - atoms * each), (0, LANES - atoms * each)))


def on_device(psi, gvec_index, vloc, beta, dmat, qmat):
    length = vloc.shape[0]
    planes = vloc.shape[1]
    width = psi.shape[2]
    blocks = lax.axis_size("pw")
    bands = lax.axis_size("band")
    chunks = round_up(width // LANES + planes, 16)
    index = gvec_index.reshape(1, width)
    mine = psi.reshape(2, width)
    atoms = jnp.concatenate([atom_blocks(dmat), atom_blocks(qmat)], axis=1)
    pay, slot = group_waves(index, mine, length, planes, chunks)
    pays = from_blocks(pay, "pw")
    sums = project(from_bands(psi, "band"), beta, bands)
    outs = lattice(pays, sums, vloc, length, planes, chunks)
    parts = [outs[0]] + [swap(outs[s], "pw", s) for s in range(1, blocks)]
    hpsi, spsi, gram = finish(parts, slot, index, mine, beta, atoms, length, planes, chunks, bands)
    return (hpsi.reshape(2, 1, width), spsi.reshape(2, 1, width), gram.reshape(2, 1, bands))


def solution(mesh):
    in_specs = (P(None, "band", "pw"), P("pw"), P(None, "pw", None), P(None, None, "pw"), P(), P())
    out_specs = (P(None, "band", "pw"), P(None, "band", "pw"), P(None, "band", None))
    return jax.shard_map(
        on_device, mesh=mesh, in_specs=in_specs, out_specs=out_specs, check_vma=False
    )
```

```python
import functools

import jax
import jax.numpy as jnp
import ml_dtypes
import numpy as np
from jax import lax
from jax.experimental import pallas as pl
from jax.experimental.pallas import tpu as pltpu
from jax.sharding import PartitionSpec as P

LANES = 128
MIB = 1024 * 1024


def cost(us):
    return pl.CostEstimate(flops=int(us * 1e9), bytes_accessed=MIB, transcendentals=0)


def round_up(value, unit):
    return -(-value // unit) * unit


def dft_parts(length):
    counter = np.arange(length)
    phase = counter[:, None] * counter[None, :] % length
    angle = phase.astype(np.float32) * np.float32(2.0 * np.pi / length)
    factor = np.float32(1.0) / np.sqrt(np.float32(length))
    return (np.cos(angle) * factor).astype(np.float32), (np.sin(angle) * factor).astype(np.float32)


def as_bf16(array):
    return np.asarray(array).astype(ml_dtypes.bfloat16)


def tables_of(length, planes, blocks):
    half = length // 2
    cosine, sine = dft_parts(length)
    rows = round_up(planes, 8)
    own = np.zeros((blocks, 2 * rows, length), np.float32)
    for block in range(blocks):
        span = slice(block * planes, (block + 1) * planes)
        own[block, :planes] = cosine[span]
        own[block, rows : rows + planes] = sine[span]
    def square(c, s, size):
        pad = ((0, size - half), (0, size - half))
        c, s = np.pad(c, pad), np.pad(s, pad)
        return np.block([[c, -s], [s, c]])

    first = slice(0, half)
    even, odd = slice(0, None, 2), slice(1, None, 2)
    along_z = np.stack(
        [
            square(cosine[even, first], -sine[even, first], LANES),
            square(cosine[odd, first], -sine[odd, first], LANES),
            square(cosine[first, even], sine[first, even], LANES),
            square(cosine[first, odd], sine[first, odd], LANES),
        ]
    )
    along_x = np.stack(
        [
            square(cosine[first, even], sine[first, even], half),
            square(cosine[first, odd], sine[first, odd], half),
            square(cosine[even, first], -sine[even, first], half),
            square(cosine[odd, first], -sine[odd, first], half),
        ]
    )
    pieces = [along_z, along_x, own]
    pieces = [np.pad(piece, ((0, 0), (0, 0), (0, 2 * LANES - piece.shape[2]))) for piece in pieces]
    return as_bf16(np.concatenate([piece.reshape(-1, 2 * LANES) for piece in pieces]))


def cell_parts(index, length):
    cell = index.astype(jnp.float32)
    x = jnp.floor((cell + 0.5) * (1.0 / (length * length)))
    rest = cell - x * (length * length)
    y = jnp.floor((rest + 0.5) * (1.0 / length))
    return x, y, rest - y * length


def iota(shape, dim):
    return lax.broadcasted_iota(jnp.int32, shape, dim).astype(jnp.float32)


def where_bf16(mask, value):
    return jnp.where(mask, value, 0.0).astype(jnp.bfloat16)


def dot(left, right):
    return jnp.dot(left, right, preferred_element_type=jnp.float32)


def dot_lanes(left, right):
    return lax.dot_general(left, right, (((1,), (1,)), ((), ())), preferred_element_type=jnp.float32)


def fetch_all(pairs, sems):
    copies = [pltpu.make_async_copy(source, target, sems.at[n]) for n, (source, target) in enumerate(pairs)]
    for copy in copies:
        copy.start()
    return copies


def group_kernel(
    length, planes, chunks, gvec_hbm, psi_hbm, pay_ref, slot_ref, hot, counts, spread, pick, gvec_ref, psi_ref, sems
):
    for copy in fetch_all(((gvec_hbm, gvec_ref), (psi_hbm, psi_ref)), sems):
        copy.wait()
    waves = gvec_ref.shape[1]
    tiles = waves // LANES
    rows = round_up(planes, 16)
    x, y, z = cell_parts(gvec_ref[...], length)
    z_half = jnp.floor(z * 0.5)
    z = z_half + (z - 2.0 * z_half) * LANES
    psi = psi_ref[...].astype(jnp.float32)
    plane = iota((rows, LANES), 0)
    for tile in range(tiles):
        span = slice(tile * LANES, (tile + 1) * LANES)
        hot[tile * rows : (tile + 1) * rows, :] = where_bf16(plane == x[:, span], 1.0)
    upto = jnp.where(iota((LANES, LANES), 0) <= iota((LANES, LANES), 1), 1.0, 0.0)
    upto = jnp.concatenate([upto, jnp.ones((LANES, LANES), jnp.float32)], axis=1)
    counts[...] = dot(hot[...], upto.astype(jnp.bfloat16))
    total = jnp.zeros((rows, LANES), jnp.float32)
    for tile in range(tiles):
        total = total + counts[tile * rows : (tile + 1) * rows, LANES:]
    need = jnp.maximum(jnp.floor((total + (LANES - 0.5)) * (1.0 / LANES)), 1.0)
    need = jnp.where(plane < planes, need, 0.0)
    below = where_bf16(iota((rows, rows), 1) < iota((rows, rows), 0), 1.0)
    first = dot(below, need.astype(jnp.bfloat16))
    ends = jnp.where((plane < planes) & (iota((rows, LANES), 1) >= first + need), 1.0, 0.0)
    chunk_plane = jnp.sum(ends, axis=0, keepdims=True)
    running = first * LANES - 1.0
    upper = iota((chunks, LANES), 0)
    lower = iota((LANES, LANES), 0)
    for tile in range(tiles):
        span = slice(tile * LANES, (tile + 1) * LANES)
        part = slice(tile * rows, (tile + 1) * rows)
        mine = plane == x[:, span]
        slot = jnp.where(mine, counts[part, :LANES] + running, 0.0)
        slot = jnp.sum(slot, axis=0, keepdims=True)
        running = running + counts[part, LANES:]
        slot_ref[:, span] = slot
        high = jnp.floor((slot + 0.5) * (1.0 / LANES))
        at_high = upper == high
        spread[0:chunks, span] = where_bf16(at_high, psi[0:1, span])
        spread[chunks : 2 * chunks, span] = where_bf16(at_high, psi[1:2, span])
        spread[2 * chunks : 3 * chunks, span] = where_bf16(at_high, y[:, span])
        spread[3 * chunks : 4 * chunks, span] = where_bf16(at_high, z[:, span])
        pick[:, span] = where_bf16(lower == slot - high * LANES, 1.0)
    pay_ref[0 : 4 * chunks, :] = dot_lanes(spread[...], pick[...]).astype(jnp.bfloat16)
    used = jnp.sum(need, axis=0, keepdims=True)
    pay_ref[4 * chunks :, :] = jnp.where(iota((16, LANES), 0) == 0.0, chunk_plane, used).astype(jnp.bfloat16)


def group_waves(index, psi, length, planes, chunks):
    waves = index.shape[1]
    rows = round_up(planes, 16)
    tiles = waves // LANES
    return pl.pallas_call(
        functools.partial(group_kernel, length, planes, chunks),
        out_shape=(
            jax.ShapeDtypeStruct((4 * chunks + 16, LANES), jnp.bfloat16),
            jax.ShapeDtypeStruct((1, waves), jnp.float32),
        ),
        scratch_shapes=[
            pltpu.VMEM((tiles * rows, LANES), jnp.bfloat16),
            pltpu.VMEM((tiles * rows, 2 * LANES), jnp.float32),
            pltpu.VMEM((4 * chunks, waves), jnp.bfloat16),
            pltpu.VMEM((LANES, waves), jnp.bfloat16),
            pltpu.VMEM((1, waves), jnp.int32),
            pltpu.VMEM((2, waves), jnp.bfloat16),
            pltpu.SemaphoreType.DMA((2,)),
        ],
        in_specs=[pl.BlockSpec(memory_space=pl.ANY)] * 2,
        compiler_params=pltpu.CompilerParams(vmem_limit_bytes=24 * MIB),
        cost_estimate=cost(3.4),
        name="group_waves",
    )(index, psi)


def lattice_kernel(length, planes, chunks, blocks, *refs):
    pays = refs[:blocks]
    sums_ref, vloc_hbm, tables = refs[blocks : blocks + 3]
    outs = refs[blocks + 3 : 2 * blocks + 3]
    wide, cells_e, cells_o, phases, vloc, result, maps, maps_s, sems, vloc_sem = refs[2 * blocks + 3 :]
    half = length // 2
    rows = round_up(planes, 8)
    both = 2 * rows
    pitch = both + 1
    spare = blocks * planes
    me = lax.axis_index("pw")
    for s in range(blocks):
        maps[s * 8 : (s + 1) * 8, :] = pays[s][4 * chunks : 4 * chunks + 16, :].astype(jnp.int32)[:8]
    (fetch,) = fetch_all(((maps, maps_s),), sems)

    def load(k, _):
        pltpu.make_async_copy(vloc_hbm.at[:, k, :], vloc.at[k], vloc_sem).start()
        return 0

    lax.fori_loop(0, planes, load, 0)
    for s in range(blocks):
        wide[s * 4 * chunks : (s + 1) * 4 * chunks, :] = pays[s][0 : 4 * chunks, :].astype(jnp.float32)
    own_at = 8 * LANES + 4 * length + pl.multiple_of(me * both, 16)
    own = tables[pl.ds(own_at, both), :][:, :length]

    def along_z(n):
        return tables[2 * LANES * n : 2 * LANES * (n + 1), :]

    def along_x(n):
        return tables[8 * LANES + length * n : 8 * LANES + length * (n + 1), :][:, :length]

    fetch.wait()
    used = maps_s[1, 0]
    for s in range(1, blocks):
        used = jnp.maximum(used, maps_s[s * 8 + 1, 0])
    level = iota((2 * LANES, LANES), 0)
    level_y = level[:length]
    group = 4 if blocks % 4 == 0 else 1
    ahead = 8 if blocks == group else 1
    batch = 8 if planes % 8 == 0 else 1
    turns = (used + ahead - 1) // ahead

    def place(s, c):
        at = maps_s[s * 8, c]
        x = (me ^ s) * planes + at
        return jnp.where(at < planes, x // 2 + x % 2 * half, spare)

    def row(s, part, c):
        return wide[pl.ds((s * 4 + part) * chunks + c, 1), :]

    def items(turn, base):
        return [(s, turn * ahead + j) for s in range(base, base + group) for j in range(ahead)]

    def pick_z(s, c):
        return where_bf16(level == row(s, 3, c), 1.0)

    def phases_of(todo):
        wanted = [where_bf16(level_y == row(s, 2, c), 1.0) for s, c in todo]
        found = []
        for n in range(0, len(todo), 2):
            both_phases = dot(own, jnp.concatenate(wanted[n : n + 2], axis=1))
            found += [both_phases[:, :LANES], both_phases[:, LANES:]][: len(wanted[n : n + 2])]
        return found

    def forward(turn, _):
        for base in range(0, blocks, group):
            todo = items(turn, base)
            found = phases_of(todo)
            mixed = []
            for (s, c), phase in zip(todo, found):
                phases[s * chunks + c] = phase.astype(jnp.bfloat16)
                re, im = row(s, 0, c), row(s, 1, c)
                cos, sin = phase[:rows], phase[rows:]
                both_parts = jnp.concatenate([re * cos - im * sin, re * sin + im * cos], axis=0)
                mixed.append(both_parts.astype(jnp.bfloat16))
            found = [dot_lanes(value, pick_z(s, c)) for (s, c), value in zip(todo, mixed)]
            spans = [place(s, c) for s, c in todo]
            for n, (s, c) in enumerate(todo):
                span = pl.ds(spans[n] * pitch, both)
                if n % ahead == 0:
                    fresh = (c == 0) | (spans[n] != place(s, jnp.maximum(c - 1, 0)))
                    before_e, before_o = cells_e[span, :], cells_o[span, :]
                else:
                    fresh = spans[n] != spans[n - 1]
                    before_e, before_o = part_e, part_o
                part_e = found[n][:, :LANES] + jnp.where(fresh, 0.0, before_e)
                part_o = found[n][:, LANES:] + jnp.where(fresh, 0.0, before_o)
                cells_e[span, :] = part_e
                cells_o[span, :] = part_o
        return 0

    lax.fori_loop(0, turns, forward, 0)
    pltpu.make_async_copy(vloc, vloc, vloc_sem).wait()

    def strided(start):
        return pl.ds(start, half, stride=pitch)

    def beside(left, right):
        return jnp.concatenate([left, right], axis=1)

    def above(upper, lower):
        return jnp.concatenate([upper, lower], axis=0)

    def middle(turn, _):
        many = [turn * batch + j for j in range(batch)]
        starts = [k + odd * half * pitch for k in many for odd in range(2)]

        def pull(cells):
            return jnp.concatenate(
                [
                    beside(cells[strided(at), :], cells[strided(at + rows), :]).astype(jnp.bfloat16)
                    for at in starts
                ],
                axis=0,
            )

        even = dot(pull(cells_e), along_z(0))
        odd = dot(pull(cells_o), along_z(1))
        low, high = (even + odd).astype(jnp.bfloat16), (even - odd).astype(jnp.bfloat16)

        def stacked(n):
            part = slice(n * half, (n + 1) * half)
            return above(
                beside(low[part, :LANES], high[part, :LANES]),
                beside(low[part, LANES:], high[part, LANES:]),
            )

        sums, differences = [], []
        for j, k in enumerate(many):
            even = dot(along_x(0), stacked(2 * j))
            odd = dot(along_x(1), stacked(2 * j + 1))
            field = vloc[k]
            field = beside(field[:, :LANES], beside(field[:, half:], field[:, : LANES - half]))
            near, far = field[:half], field[half:]
            first = (even + odd) * above(near, near)
            second = (even - odd) * above(far, far)
            for table, value in ((along_x(2), first + second), (along_x(3), first - second)):
                back = dot(table, value.astype(jnp.bfloat16))
                total, change = back[:, :LANES] + back[:, LANES:], back[:, :LANES] - back[:, LANES:]
                sums.append(beside(total[:half], total[half:]).astype(jnp.bfloat16))
                differences.append(beside(change[:half], change[half:]).astype(jnp.bfloat16))
        even = dot(jnp.concatenate(sums, axis=0), along_z(2))
        odd = dot(jnp.concatenate(differences, axis=0), along_z(3))
        for n, at in enumerate(starts):
            part = slice(n * half, (n + 1) * half)
            cells_e[strided(at), :] = even[part, :LANES]
            cells_e[strided(at + rows), :] = even[part, LANES:]
            cells_o[strided(at), :] = odd[part, :LANES]
            cells_o[strided(at + rows), :] = odd[part, LANES:]
        return 0

    lax.fori_loop(0, planes // batch, middle, 0)

    def backward(turn, _):
        for base in range(0, blocks, group):
            todo = items(turn, base)
            found = []
            for s, c in todo:
                span = pl.ds(place(s, c) * pitch, both)
                value = beside(cells_e[span, :], cells_o[span, :]).astype(jnp.bfloat16)
                found.append(dot(value, pick_z(s, c)))
            for (s, c), part in zip(todo, found):
                phase = phases[s * chunks + c].astype(jnp.float32)
                re, im = part[:rows], part[rows:]
                cos, sin = phase[:rows], phase[rows:]
                result[pl.ds(s * 2 * chunks + c, 1), :] = jnp.sum(re * cos + im * sin, axis=0, keepdims=True)
                result[pl.ds((s * 2 + 1) * chunks + c, 1), :] = jnp.sum(im * cos - re * sin, axis=0, keepdims=True)
        return 0

    spare_span = pl.ds(spare * pitch, both)
    cells_e[spare_span, :] = jnp.zeros((both, LANES), jnp.float32)
    cells_o[spare_span, :] = jnp.zeros((both, LANES), jnp.float32)
    result[...] = jnp.zeros_like(result)
    lax.fori_loop(0, turns, backward, 0)
    rest = sums_ref[...]
    pieces = []
    for _ in range(3):
        pieces.append(rest.astype(jnp.bfloat16))
        rest = rest - pieces[-1].astype(jnp.float32)
    size = sums_ref.shape[0]
    for s in range(blocks):
        outs[s][0 : 2 * chunks, :] = result[s * 2 * chunks : (s + 1) * 2 * chunks, :].astype(jnp.bfloat16)
        for n, piece in enumerate(pieces):
            outs[s][2 * chunks + n * size : 2 * chunks + (n + 1) * size, :] = piece


def lattice(pays, sums, vloc, length, planes, chunks):
    blocks = len(pays)
    rows = round_up(planes, 8)
    tables = tables_of(length, planes, blocks)
    vmem = pl.BlockSpec(memory_space=pltpu.VMEM)
    return pl.pallas_call(
        functools.partial(lattice_kernel, length, planes, chunks, blocks),
        out_shape=[jax.ShapeDtypeStruct((2 * chunks + 3 * sums.shape[0], LANES), jnp.bfloat16)] * blocks,
        in_specs=[vmem] * (blocks + 1) + [pl.BlockSpec(memory_space=pl.ANY), vmem],
        out_specs=[vmem] * blocks,
        scratch_shapes=[
            pltpu.VMEM((blocks * 4 * chunks, LANES), jnp.float32),
            pltpu.VMEM((round_up((blocks * planes + 1) * (2 * rows + 1), 8), LANES), jnp.float32),
            pltpu.VMEM((round_up((blocks * planes + 1) * (2 * rows + 1), 8), LANES), jnp.float32),
            pltpu.VMEM((blocks * chunks, 2 * rows, LANES), jnp.bfloat16),
            pltpu.VMEM((planes, length, length), jnp.float32),
            pltpu.VMEM((blocks * 2 * chunks, LANES), jnp.float32),
            pltpu.VMEM((blocks * 8, LANES), jnp.int32),
            pltpu.SMEM((blocks * 8, LANES), jnp.int32),
            pltpu.SemaphoreType.DMA((1,)),
            pltpu.SemaphoreType.DMA,
        ],
        compiler_params=pltpu.CompilerParams(vmem_limit_bytes=48 * MIB),
        cost_estimate=cost(36.0),
        name="lattice",
    )(*pays, sums, vloc, tables)


def project_kernel(bands, *refs):
    beta_hbm, out_ref, beta_ref, sems = refs[-4:]
    (fetch,) = fetch_all(((beta_hbm, beta_ref),), sems)
    every = [ref[...].astype(jnp.float32) for ref in refs[:-4]]
    count = beta_ref.shape[1]
    rows = out_ref.shape[0] // 2
    pad = [jnp.zeros((rows - bands, every[0].shape[2]), jnp.float32)] if rows > bands else []
    re = jnp.concatenate([value[0] for value in every] + pad, axis=0)
    im = jnp.concatenate([value[1] for value in every] + pad, axis=0)
    fetch.wait()
    stack = jnp.concatenate([re, im], axis=0).astype(jnp.bfloat16)
    on_re, on_im = dot_lanes(beta_ref[0], stack), dot_lanes(beta_ref[1], stack)
    found = jnp.concatenate([on_re[:, :rows] + on_im[:, rows:], on_re[:, rows:] - on_im[:, :rows]], axis=1)
    out_ref[...] = jnp.zeros_like(out_ref)
    out_ref[:, :count] = found.T
    own_re, own_im = re[:1], im[:1]
    over = jnp.concatenate(
        [
            jnp.sum(re * own_re + im * own_im, axis=1, keepdims=True),
            jnp.sum(im * own_re - re * own_im, axis=1, keepdims=True),
        ],
        axis=0,
    )
    out_ref[...] = jnp.where(iota(out_ref.shape, 1) == count, over, out_ref[...])


def project(every, beta, bands):
    return pl.pallas_call(
        functools.partial(project_kernel, bands),
        out_shape=jax.ShapeDtypeStruct((2 * round_up(bands, 8), LANES), jnp.float32),
        in_specs=[pl.BlockSpec(memory_space=pltpu.VMEM)] * len(every) + [pl.BlockSpec(memory_space=pl.ANY)],
        scratch_shapes=[pltpu.VMEM(beta.shape, beta.dtype), pltpu.SemaphoreType.DMA((1,))],
        compiler_params=pltpu.CompilerParams(vmem_limit_bytes=16 * MIB),
        cost_estimate=cost(1.2),
        name="project",
    )(*every, beta)


def finish_kernel(length, planes, chunks, blocks, bands, *refs):
    parts = refs[:blocks]
    slot_ref, gvec_ref, psi_ref, beta_ref, atoms_ref, hpsi_ref, spsi_ref, gram_ref = refs[blocks:]
    waves = slot_ref.shape[1]
    count = beta_ref.shape[1]
    total = parts[0][...].astype(jnp.float32)
    for part in parts[1:]:
        total = total + part[...].astype(jnp.float32)
    size = (total.shape[0] - 2 * chunks) // 3
    half_size = size // 2
    sums = [total[2 * chunks + n * size : 2 * chunks + (n + 1) * size] for n in range(3)]
    sums = sums[0] + (sums[1] + sums[2])
    coef = jnp.dot(sums, atoms_ref[...], precision=lax.Precision.HIGHEST, preferred_element_type=jnp.float32)
    coef = coef.astype(jnp.bfloat16).astype(jnp.float32)
    d_re, d_im = coef[:1, :count], coef[half_size : half_size + 1, :count]
    q_re, q_im = coef[:1, LANES : LANES + count], coef[half_size : half_size + 1, LANES : LANES + count]
    none = jnp.zeros((4, count), jnp.float32)
    on_re = jnp.concatenate([d_re, d_im, q_re, q_im, none], axis=0).astype(jnp.bfloat16)
    on_im = jnp.concatenate([-d_im, d_re, -q_im, q_re, none], axis=0).astype(jnp.bfloat16)
    added = dot(on_re, beta_ref[0]) + dot(on_im, beta_ref[1])

    own_re, own_im = sums[:1], sums[half_size : half_size + 1]
    each_re, each_im = coef[:half_size, LANES:], coef[half_size:, LANES:]
    over = iota((half_size, LANES), 1) == count
    gram_re = own_re * each_re + own_im * each_im + jnp.where(over, sums[:half_size], 0.0)
    gram_im = own_re * each_im - own_im * each_re + jnp.where(over, sums[half_size:], 0.0)
    slot_at = lax.broadcasted_iota(jnp.int32, (half_size, bands), 0)
    if doubles(bands):
        turn = lax.axis_index("band") ^ slot_at
    else:
        turn = lax.axis_index("band") - slot_at
        turn = jnp.where(turn < 0, turn + bands, turn)
    here = turn == lax.broadcasted_iota(jnp.int32, (half_size, bands), 1)
    here = here & (lax.broadcasted_iota(jnp.int32, (half_size, bands), 0) < bands)
    for n, value in enumerate((gram_re, gram_im)):
        value = jnp.sum(value, axis=1, keepdims=True)
        value = jnp.sum(jnp.where(here, value, 0.0), axis=0, keepdims=True)
        gram_ref[n : n + 1, :] = value * (1.0 / (waves * blocks))

    local = total[: 2 * chunks]
    turned = jnp.concatenate([local[:chunks].T, local[chunks:].T], axis=0).astype(jnp.bfloat16)
    x, y, z = cell_parts(gvec_ref[...], length)
    x = x + (lax.axis_index("pw") * planes).astype(jnp.float32)

    def fold(level):
        return jnp.where(level < length // 2, level, level - length)

    x, y, z = fold(x), fold(y), fold(z)
    kinetic = 4.0 * (x * x + y * y + z * z) / (length * length)
    slot = slot_ref[...]
    high = jnp.floor((slot + 0.5) * (1.0 / LANES))
    low = slot - high * LANES
    for tile in range(waves // LANES):
        span = slice(tile * LANES, (tile + 1) * LANES)
        at_high = where_bf16(iota((chunks, LANES), 0) == high[:, span], 1.0)
        rows = dot(turned, at_high)
        mine = iota((LANES, LANES), 0) == low[:, span]
        re = jnp.sum(jnp.where(mine, rows[:LANES], 0.0), axis=0, keepdims=True)
        im = jnp.sum(jnp.where(mine, rows[LANES:], 0.0), axis=0, keepdims=True)
        both = jnp.concatenate([re, im], axis=0)
        psi = psi_ref[:, span].astype(jnp.float32)
        hpsi_ref[:, span] = (both + kinetic[:, span] * psi + added[0:2, span]).astype(jnp.bfloat16)
        spsi_ref[:, span] = (psi + added[2:4, span]).astype(jnp.bfloat16)


def finish(parts, slot, index, psi, beta, atoms, length, planes, chunks, bands):
    blocks = len(parts)
    return pl.pallas_call(
        functools.partial(finish_kernel, length, planes, chunks, blocks, bands),
        out_shape=(
            jax.ShapeDtypeStruct(psi.shape, jnp.bfloat16),
            jax.ShapeDtypeStruct(psi.shape, jnp.bfloat16),
            jax.ShapeDtypeStruct((2, bands), jnp.float32),
        ),
        compiler_params=pltpu.CompilerParams(vmem_limit_bytes=16 * MIB),
        cost_estimate=cost(2.1),
        name="finish",
    )(*parts, slot, index, psi, beta, atoms)


def swap(value, axis, step):
    size = lax.axis_size(axis)
    return lax.ppermute(value, axis, [(k, k ^ step) for k in range(size)])


def doubles(size):
    return size & (size - 1) == 0


def from_blocks(value, axis):
    size = lax.axis_size(axis)
    found = {0: value}
    step = size // 2
    while step:
        found.update({s + step: swap(found[s], axis, step) for s in list(found)})
        step //= 2
    return [found[s] for s in range(size)]


def from_bands(value, axis, after):
    size = lax.axis_size(axis)
    if not doubles(size):
        pairs = [[(k, (k + s) % size) for k in range(size)] for s in range(1, size)]
        held = [value] + [lax.ppermute(value, axis, pair) for pair in pairs]
        return [part[:, None] for part in held]
    other = swap(value, axis, 1) if size > 1 else value
    other, _ = lax.optimization_barrier((other, after))
    held = [value[:, None], other[:, None]][:size]
    step = 2
    while step < size:
        value = jnp.concatenate(held, axis=1)
        held = [value, swap(value, axis, step)]
        step *= 2
    return held


def atom_blocks(matrix):
    atoms, each = matrix.shape[0], matrix.shape[1]
    same = jnp.eye(atoms, dtype=matrix.dtype)[:, None, :, None]
    square = (same * jnp.transpose(matrix, (0, 2, 1))[:, :, None, :]).reshape(atoms * each, atoms * each)
    return jnp.pad(square, ((0, LANES - atoms * each), (0, LANES - atoms * each)))


def on_device(psi, gvec_index, vloc, beta, dmat, qmat):
    length = vloc.shape[0]
    planes = vloc.shape[1]
    width = psi.shape[2]
    blocks = lax.axis_size("pw")
    bands = lax.axis_size("band")
    chunks = round_up(width // LANES + planes, 16)
    index = gvec_index.reshape(1, width)
    mine = psi.reshape(2, width)
    pay, slot = group_waves(index, mine, length, planes, chunks)
    pays = from_blocks(pay, "pw")
    sums = project(from_bands(mine, "band", pay), beta, bands)
    outs = lattice(pays, sums, vloc, length, planes, chunks)
    dmat, qmat, _ = lax.optimization_barrier((dmat, qmat, outs[0]))
    atoms = jnp.concatenate([atom_blocks(dmat), atom_blocks(qmat)], axis=1)
    parts = [outs[0]] + [swap(outs[s], "pw", s) for s in range(1, blocks)]
    hpsi, spsi, gram = finish(parts, slot, index, mine, beta, atoms, length, planes, chunks, bands)
    return (hpsi.reshape(2, 1, width), spsi.reshape(2, 1, width), gram.reshape(2, 1, bands))


def solution(mesh):
    in_specs = (P(None, "band", "pw"), P("pw"), P(None, "pw", None), P(None, None, "pw"), P(), P())
    out_specs = (P(None, "band", "pw"), P(None, "band", "pw"), P(None, "band", None))
    return jax.shard_map(
        on_device, mesh=mesh, in_specs=in_specs, out_specs=out_specs, check_vma=False
    )
```

```python
import functools

import jax
import jax.numpy as jnp
import ml_dtypes
import numpy as np
from jax import lax
from jax.experimental import pallas as pl
from jax.experimental.pallas import tpu as pltpu
from jax.sharding import PartitionSpec as P

LANES = 128
MIB = 1024 * 1024


def cost(us):
    return pl.CostEstimate(flops=int(us * 1e9), bytes_accessed=MIB, transcendentals=0)


def round_up(value, unit):
    return -(-value // unit) * unit


def dft_parts(length):
    counter = np.arange(length)
    phase = counter[:, None] * counter[None, :] % length
    angle = phase.astype(np.float32) * np.float32(2.0 * np.pi / length)
    factor = np.float32(1.0) / np.sqrt(np.float32(length))
    return (np.cos(angle) * factor).astype(np.float32), (np.sin(angle) * factor).astype(np.float32)


def as_bf16(array):
    return np.asarray(array).astype(ml_dtypes.bfloat16)


def tables_of(length, planes, blocks):
    half = length // 2
    cosine, sine = dft_parts(length)
    rows = round_up(planes, 8)
    own = np.zeros((blocks, 2 * rows, length), np.float32)
    for block in range(blocks):
        span = slice(block * planes, (block + 1) * planes)
        own[block, :planes] = cosine[span]
        own[block, rows : rows + planes] = sine[span]
    def square(c, s, size):
        pad = ((0, size - half), (0, size - half))
        c, s = np.pad(c, pad), np.pad(s, pad)
        return np.block([[c, -s], [s, c]])

    first = slice(0, half)
    even, odd = slice(0, None, 2), slice(1, None, 2)
    along_z = np.stack(
        [
            square(cosine[even, first], -sine[even, first], LANES),
            square(cosine[odd, first], -sine[odd, first], LANES),
            square(cosine[first, even], sine[first, even], LANES),
            square(cosine[first, odd], sine[first, odd], LANES),
        ]
    )
    along_x = np.stack(
        [
            square(cosine[first, even], sine[first, even], half),
            square(cosine[first, odd], sine[first, odd], half),
            square(cosine[even, first], -sine[even, first], half),
            square(cosine[odd, first], -sine[odd, first], half),
        ]
    )
    pieces = [along_z, along_x, own]
    pieces = [np.pad(piece, ((0, 0), (0, 0), (0, 2 * LANES - piece.shape[2]))) for piece in pieces]
    return as_bf16(np.concatenate([piece.reshape(-1, 2 * LANES) for piece in pieces]))


def cell_parts(index, length):
    cell = index.astype(jnp.float32)
    x = jnp.floor((cell + 0.5) * (1.0 / (length * length)))
    rest = cell - x * (length * length)
    y = jnp.floor((rest + 0.5) * (1.0 / length))
    return x, y, rest - y * length


def iota(shape, dim):
    return lax.broadcasted_iota(jnp.int32, shape, dim).astype(jnp.float32)


def where_bf16(mask, value):
    return jnp.where(mask, value, 0.0).astype(jnp.bfloat16)


def dot(left, right):
    return jnp.dot(left, right, preferred_element_type=jnp.float32)


def dot_lanes(left, right):
    return lax.dot_general(left, right, (((1,), (1,)), ((), ())), preferred_element_type=jnp.float32)


def fetch_all(pairs, sems):
    copies = [pltpu.make_async_copy(source, target, sems.at[n]) for n, (source, target) in enumerate(pairs)]
    for copy in copies:
        copy.start()
    return copies


def group_kernel(
    length, planes, chunks, gvec_hbm, psi_hbm, pay_ref, slot_ref, hot, counts, spread, pick, gvec_ref, psi_ref, sems
):
    for copy in fetch_all(((gvec_hbm, gvec_ref), (psi_hbm, psi_ref)), sems):
        copy.wait()
    waves = gvec_ref.shape[1]
    tiles = waves // LANES
    rows = round_up(planes, 16)
    x, y, z = cell_parts(gvec_ref[...], length)
    z_half = jnp.floor(z * 0.5)
    z = z_half + (z - 2.0 * z_half) * LANES
    psi = psi_ref[...].astype(jnp.float32)
    plane = iota((rows, LANES), 0)
    for tile in range(tiles):
        span = slice(tile * LANES, (tile + 1) * LANES)
        hot[tile * rows : (tile + 1) * rows, :] = where_bf16(plane == x[:, span], 1.0)
    upto = jnp.where(iota((LANES, LANES), 0) <= iota((LANES, LANES), 1), 1.0, 0.0)
    upto = jnp.concatenate([upto, jnp.ones((LANES, LANES), jnp.float32)], axis=1)
    counts[...] = dot(hot[...], upto.astype(jnp.bfloat16))
    total = jnp.zeros((rows, LANES), jnp.float32)
    for tile in range(tiles):
        total = total + counts[tile * rows : (tile + 1) * rows, LANES:]
    need = jnp.maximum(jnp.floor((total + (LANES - 0.5)) * (1.0 / LANES)), 1.0)
    need = jnp.where(plane < planes, need, 0.0)
    below = where_bf16(iota((rows, rows), 1) < iota((rows, rows), 0), 1.0)
    first = dot(below, need.astype(jnp.bfloat16))
    ends = jnp.where((plane < planes) & (iota((rows, LANES), 1) >= first + need), 1.0, 0.0)
    chunk_plane = jnp.sum(ends, axis=0, keepdims=True)
    running = first * LANES - 1.0
    upper = iota((chunks, LANES), 0)
    lower = iota((LANES, LANES), 0)
    for tile in range(tiles):
        span = slice(tile * LANES, (tile + 1) * LANES)
        part = slice(tile * rows, (tile + 1) * rows)
        mine = plane == x[:, span]
        slot = jnp.where(mine, counts[part, :LANES] + running, 0.0)
        slot = jnp.sum(slot, axis=0, keepdims=True)
        running = running + counts[part, LANES:]
        slot_ref[:, span] = slot
        high = jnp.floor((slot + 0.5) * (1.0 / LANES))
        at_high = upper == high
        spread[0:chunks, span] = where_bf16(at_high, psi[0:1, span])
        spread[chunks : 2 * chunks, span] = where_bf16(at_high, psi[1:2, span])
        spread[2 * chunks : 3 * chunks, span] = where_bf16(at_high, y[:, span])
        spread[3 * chunks : 4 * chunks, span] = where_bf16(at_high, z[:, span])
        pick[:, span] = where_bf16(lower == slot - high * LANES, 1.0)
    pay_ref[0 : 4 * chunks, :] = dot_lanes(spread[...], pick[...]).astype(jnp.bfloat16)
    used = jnp.sum(need, axis=0, keepdims=True)
    pay_ref[4 * chunks :, :] = jnp.where(iota((16, LANES), 0) == 0.0, chunk_plane, used).astype(jnp.bfloat16)


def group_waves(index, psi, length, planes, chunks):
    waves = index.shape[1]
    rows = round_up(planes, 16)
    tiles = waves // LANES
    return pl.pallas_call(
        functools.partial(group_kernel, length, planes, chunks),
        out_shape=(
            jax.ShapeDtypeStruct((4 * chunks + 16, LANES), jnp.bfloat16),
            jax.ShapeDtypeStruct((1, waves), jnp.float32),
        ),
        scratch_shapes=[
            pltpu.VMEM((tiles * rows, LANES), jnp.bfloat16),
            pltpu.VMEM((tiles * rows, 2 * LANES), jnp.float32),
            pltpu.VMEM((4 * chunks, waves), jnp.bfloat16),
            pltpu.VMEM((LANES, waves), jnp.bfloat16),
            pltpu.VMEM((1, waves), jnp.int32),
            pltpu.VMEM((2, waves), jnp.bfloat16),
            pltpu.SemaphoreType.DMA((2,)),
        ],
        in_specs=[pl.BlockSpec(memory_space=pl.ANY)] * 2,
        compiler_params=pltpu.CompilerParams(vmem_limit_bytes=24 * MIB),
        cost_estimate=cost(3.4),
        name="group_waves",
    )(index, psi)


def lattice_kernel(length, planes, chunks, blocks, *refs):
    pays = refs[:blocks]
    sums_ref, vloc_hbm, tables = refs[blocks : blocks + 3]
    outs = refs[blocks + 3 : 2 * blocks + 3]
    wide, cells_e, cells_o, phases, vloc, result, maps, maps_s, sems, vloc_sem = refs[2 * blocks + 3 :]
    half = length // 2
    rows = round_up(planes, 8)
    both = 2 * rows
    pitch = both + 1
    spare = blocks * planes
    me = lax.axis_index("pw")
    for s in range(blocks):
        maps[s * 8 : (s + 1) * 8, :] = pays[s][4 * chunks : 4 * chunks + 16, :].astype(jnp.int32)[:8]
    (fetch,) = fetch_all(((maps, maps_s),), sems)

    def load(k, _):
        pltpu.make_async_copy(vloc_hbm.at[:, k, :], vloc.at[k], vloc_sem).start()
        return 0

    lax.fori_loop(0, planes, load, 0)
    for s in range(blocks):
        wide[s * 4 * chunks : (s + 1) * 4 * chunks, :] = pays[s][0 : 4 * chunks, :].astype(jnp.float32)
    own_at = 8 * LANES + 4 * length + pl.multiple_of(me * both, 16)
    own = tables[pl.ds(own_at, both), :][:, :length]

    def along_z(n):
        return tables[2 * LANES * n : 2 * LANES * (n + 1), :]

    def along_x(n):
        return tables[8 * LANES + length * n : 8 * LANES + length * (n + 1), :][:, :length]

    fetch.wait()
    used = maps_s[1, 0]
    for s in range(1, blocks):
        used = jnp.maximum(used, maps_s[s * 8 + 1, 0])
    level = iota((2 * LANES, LANES), 0)
    level_y = level[:length]
    group = 4 if blocks % 4 == 0 else 1
    ahead = 8 if blocks == group else 1
    batch = 16 if planes % 16 == 0 else 1
    turns = (used + ahead - 1) // ahead

    def place(s, c):
        at = maps_s[s * 8, c]
        x = (me ^ s) * planes + at
        return jnp.where(at < planes, x // 2 + x % 2 * half, spare)

    def row(s, part, c):
        return wide[pl.ds((s * 4 + part) * chunks + c, 1), :]

    def items(turn, base):
        return [(s, turn * ahead + j) for s in range(base, base + group) for j in range(ahead)]

    def pick_z(s, c):
        return where_bf16(level == row(s, 3, c), 1.0)

    def phases_of(todo):
        wanted = [where_bf16(level_y == row(s, 2, c), 1.0) for s, c in todo]
        found = []
        for n in range(0, len(todo), 2):
            both_phases = dot(own, jnp.concatenate(wanted[n : n + 2], axis=1))
            found += [both_phases[:, :LANES], both_phases[:, LANES:]][: len(wanted[n : n + 2])]
        return found

    def forward(turn, _):
        for base in range(0, blocks, group):
            todo = items(turn, base)
            found = phases_of(todo)
            mixed = []
            for (s, c), phase in zip(todo, found):
                phases[s * chunks + c] = phase.astype(jnp.bfloat16)
                re, im = row(s, 0, c), row(s, 1, c)
                cos, sin = phase[:rows], phase[rows:]
                both_parts = jnp.concatenate([re * cos - im * sin, re * sin + im * cos], axis=0)
                mixed.append(both_parts.astype(jnp.bfloat16))
            found = [dot_lanes(value, pick_z(s, c)) for (s, c), value in zip(todo, mixed)]
            spans = [place(s, c) for s, c in todo]
            for n, (s, c) in enumerate(todo):
                span = pl.ds(spans[n] * pitch, both)
                if n % ahead == 0:
                    fresh = (c == 0) | (spans[n] != place(s, jnp.maximum(c - 1, 0)))
                    before_e, before_o = cells_e[span, :], cells_o[span, :]
                else:
                    fresh = spans[n] != spans[n - 1]
                    before_e, before_o = part_e, part_o
                part_e = found[n][:, :LANES] + jnp.where(fresh, 0.0, before_e)
                part_o = found[n][:, LANES:] + jnp.where(fresh, 0.0, before_o)
                cells_e[span, :] = part_e
                cells_o[span, :] = part_o
        return 0

    lax.fori_loop(0, turns, forward, 0)
    pltpu.make_async_copy(vloc, vloc, vloc_sem).wait()

    def strided(start):
        return pl.ds(start, half, stride=pitch)

    def beside(left, right):
        return jnp.concatenate([left, right], axis=1)

    def above(upper, lower):
        return jnp.concatenate([upper, lower], axis=0)

    def middle(turn, _):
        many = [turn * batch + j for j in range(batch)]
        starts = [k + odd * half * pitch for k in many for odd in range(2)]

        def pull(cells):
            return jnp.concatenate(
                [
                    beside(cells[strided(at), :], cells[strided(at + rows), :]).astype(jnp.bfloat16)
                    for at in starts
                ],
                axis=0,
            )

        even = dot(pull(cells_e), along_z(0))
        odd = dot(pull(cells_o), along_z(1))
        low, high = (even + odd).astype(jnp.bfloat16), (even - odd).astype(jnp.bfloat16)

        def stacked(n):
            part = slice(n * half, (n + 1) * half)
            return above(
                beside(low[part, :LANES], high[part, :LANES]),
                beside(low[part, LANES:], high[part, LANES:]),
            )

        sums, differences = [], []
        for j, k in enumerate(many):
            even = dot(along_x(0), stacked(2 * j))
            odd = dot(along_x(1), stacked(2 * j + 1))
            field = vloc[k]
            field = beside(field[:, :LANES], beside(field[:, half:], field[:, : LANES - half]))
            near, far = field[:half], field[half:]
            first = (even + odd) * above(near, near)
            second = (even - odd) * above(far, far)
            for table, value in ((along_x(2), first + second), (along_x(3), first - second)):
                back = dot(table, value.astype(jnp.bfloat16))
                total, change = back[:, :LANES] + back[:, LANES:], back[:, :LANES] - back[:, LANES:]
                sums.append(beside(total[:half], total[half:]).astype(jnp.bfloat16))
                differences.append(beside(change[:half], change[half:]).astype(jnp.bfloat16))
        even = dot(jnp.concatenate(sums, axis=0), along_z(2))
        odd = dot(jnp.concatenate(differences, axis=0), along_z(3))
        for n, at in enumerate(starts):
            part = slice(n * half, (n + 1) * half)
            cells_e[strided(at), :] = even[part, :LANES]
            cells_e[strided(at + rows), :] = even[part, LANES:]
            cells_o[strided(at), :] = odd[part, :LANES]
            cells_o[strided(at + rows), :] = odd[part, LANES:]
        return 0

    lax.fori_loop(0, planes // batch, middle, 0)

    def backward(turn, _):
        for base in range(0, blocks, group):
            todo = items(turn, base)
            found = []
            for s, c in todo:
                span = pl.ds(place(s, c) * pitch, both)
                value = beside(cells_e[span, :], cells_o[span, :]).astype(jnp.bfloat16)
                found.append(dot(value, pick_z(s, c)))
            for (s, c), part in zip(todo, found):
                phase = phases[s * chunks + c].astype(jnp.float32)
                re, im = part[:rows], part[rows:]
                cos, sin = phase[:rows], phase[rows:]
                result[pl.ds(s * 2 * chunks + c, 1), :] = jnp.sum(re * cos + im * sin, axis=0, keepdims=True)
                result[pl.ds((s * 2 + 1) * chunks + c, 1), :] = jnp.sum(im * cos - re * sin, axis=0, keepdims=True)
        return 0

    spare_span = pl.ds(spare * pitch, both)
    cells_e[spare_span, :] = jnp.zeros((both, LANES), jnp.float32)
    cells_o[spare_span, :] = jnp.zeros((both, LANES), jnp.float32)
    result[...] = jnp.zeros_like(result)
    lax.fori_loop(0, turns, backward, 0)
    rest = sums_ref[...]
    pieces = []
    for _ in range(3):
        pieces.append(rest.astype(jnp.bfloat16))
        rest = rest - pieces[-1].astype(jnp.float32)
    size = sums_ref.shape[0]
    for s in range(blocks):
        outs[s][0 : 2 * chunks, :] = result[s * 2 * chunks : (s + 1) * 2 * chunks, :].astype(jnp.bfloat16)
        for n, piece in enumerate(pieces):
            outs[s][2 * chunks + n * size : 2 * chunks + (n + 1) * size, :] = piece


def lattice(pays, sums, vloc, length, planes, chunks):
    blocks = len(pays)
    rows = round_up(planes, 8)
    tables = tables_of(length, planes, blocks)
    vmem = pl.BlockSpec(memory_space=pltpu.VMEM)
    return pl.pallas_call(
        functools.partial(lattice_kernel, length, planes, chunks, blocks),
        out_shape=[jax.ShapeDtypeStruct((2 * chunks + 3 * sums.shape[0], LANES), jnp.bfloat16)] * blocks,
        in_specs=[vmem] * (blocks + 1) + [pl.BlockSpec(memory_space=pl.ANY), vmem],
        out_specs=[vmem] * blocks,
        scratch_shapes=[
            pltpu.VMEM((blocks * 4 * chunks, LANES), jnp.float32),
            pltpu.VMEM((round_up((blocks * planes + 1) * (2 * rows + 1), 8), LANES), jnp.float32),
            pltpu.VMEM((round_up((blocks * planes + 1) * (2 * rows + 1), 8), LANES), jnp.float32),
            pltpu.VMEM((blocks * chunks, 2 * rows, LANES), jnp.bfloat16),
            pltpu.VMEM((planes, length, length), jnp.float32),
            pltpu.VMEM((blocks * 2 * chunks, LANES), jnp.float32),
            pltpu.VMEM((blocks * 8, LANES), jnp.int32),
            pltpu.SMEM((blocks * 8, LANES), jnp.int32),
            pltpu.SemaphoreType.DMA((1,)),
            pltpu.SemaphoreType.DMA,
        ],
        compiler_params=pltpu.CompilerParams(vmem_limit_bytes=48 * MIB),
        cost_estimate=cost(36.0),
        name="lattice",
    )(*pays, sums, vloc, tables)


def project_kernel(bands, *refs):
    beta_hbm, out_ref, beta_ref, sems = refs[-4:]
    (fetch,) = fetch_all(((beta_hbm, beta_ref),), sems)
    every = [ref[...].astype(jnp.float32) for ref in refs[:-4]]
    count = beta_ref.shape[1]
    rows = out_ref.shape[0] // 2
    pad = [jnp.zeros((rows - bands, every[0].shape[2]), jnp.float32)] if rows > bands else []
    re = jnp.concatenate([value[0] for value in every] + pad, axis=0)
    im = jnp.concatenate([value[1] for value in every] + pad, axis=0)
    fetch.wait()
    stack = jnp.concatenate([re, im], axis=0).astype(jnp.bfloat16)
    on_re, on_im = dot_lanes(beta_ref[0], stack), dot_lanes(beta_ref[1], stack)
    found = jnp.concatenate([on_re[:, :rows] + on_im[:, rows:], on_re[:, rows:] - on_im[:, :rows]], axis=1)
    out_ref[...] = jnp.zeros_like(out_ref)
    out_ref[:, :count] = found.T
    own_re, own_im = re[:1], im[:1]
    over = jnp.concatenate(
        [
            jnp.sum(re * own_re + im * own_im, axis=1, keepdims=True),
            jnp.sum(im * own_re - re * own_im, axis=1, keepdims=True),
        ],
        axis=0,
    )
    out_ref[...] = jnp.where(iota(out_ref.shape, 1) == count, over, out_ref[...])


def project(every, beta, bands):
    return pl.pallas_call(
        functools.partial(project_kernel, bands),
        out_shape=jax.ShapeDtypeStruct((2 * round_up(bands, 8), LANES), jnp.float32),
        in_specs=[pl.BlockSpec(memory_space=pltpu.VMEM)] * len(every) + [pl.BlockSpec(memory_space=pl.ANY)],
        scratch_shapes=[pltpu.VMEM(beta.shape, beta.dtype), pltpu.SemaphoreType.DMA((1,))],
        compiler_params=pltpu.CompilerParams(vmem_limit_bytes=16 * MIB),
        cost_estimate=cost(1.2),
        name="project",
    )(*every, beta)


def finish_kernel(length, planes, chunks, blocks, bands, *refs):
    parts = refs[:blocks]
    slot_ref, gvec_ref, psi_ref, beta_ref, atoms_ref, hpsi_ref, spsi_ref, gram_ref = refs[blocks:]
    waves = slot_ref.shape[1]
    count = beta_ref.shape[1]
    total = parts[0][...].astype(jnp.float32)
    for part in parts[1:]:
        total = total + part[...].astype(jnp.float32)
    size = (total.shape[0] - 2 * chunks) // 3
    half_size = size // 2
    sums = [total[2 * chunks + n * size : 2 * chunks + (n + 1) * size] for n in range(3)]
    sums = sums[0] + (sums[1] + sums[2])
    coef = jnp.dot(sums, atoms_ref[...], precision=lax.Precision.HIGHEST, preferred_element_type=jnp.float32)
    coef = coef.astype(jnp.bfloat16).astype(jnp.float32)
    d_re, d_im = coef[:1, :count], coef[half_size : half_size + 1, :count]
    q_re, q_im = coef[:1, LANES : LANES + count], coef[half_size : half_size + 1, LANES : LANES + count]
    none = jnp.zeros((4, count), jnp.float32)
    on_re = jnp.concatenate([d_re, d_im, q_re, q_im, none], axis=0).astype(jnp.bfloat16)
    on_im = jnp.concatenate([-d_im, d_re, -q_im, q_re, none], axis=0).astype(jnp.bfloat16)
    added = dot(on_re, beta_ref[0]) + dot(on_im, beta_ref[1])

    own_re, own_im = sums[:1], sums[half_size : half_size + 1]
    each_re, each_im = coef[:half_size, LANES:], coef[half_size:, LANES:]
    over = iota((half_size, LANES), 1) == count
    gram_re = own_re * each_re + own_im * each_im + jnp.where(over, sums[:half_size], 0.0)
    gram_im = own_re * each_im - own_im * each_re + jnp.where(over, sums[half_size:], 0.0)
    slot_at = lax.broadcasted_iota(jnp.int32, (half_size, bands), 0)
    if doubles(bands):
        turn = lax.axis_index("band")
        for place, step in enumerate(doubling_steps(bands)):
            turn = turn ^ (((slot_at >> place) & 1) * step)
    else:
        turn = lax.axis_index("band") - slot_at
        turn = jnp.where(turn < 0, turn + bands, turn)
    here = turn == lax.broadcasted_iota(jnp.int32, (half_size, bands), 1)
    here = here & (lax.broadcasted_iota(jnp.int32, (half_size, bands), 0) < bands)
    for n, value in enumerate((gram_re, gram_im)):
        value = jnp.sum(value, axis=1, keepdims=True)
        value = jnp.sum(jnp.where(here, value, 0.0), axis=0, keepdims=True)
        gram_ref[n : n + 1, :] = value * (1.0 / (waves * blocks))

    local = total[: 2 * chunks]
    turned = jnp.concatenate([local[:chunks].T, local[chunks:].T], axis=0).astype(jnp.bfloat16)
    x, y, z = cell_parts(gvec_ref[...], length)
    x = x + (lax.axis_index("pw") * planes).astype(jnp.float32)

    def fold(level):
        return jnp.where(level < length // 2, level, level - length)

    x, y, z = fold(x), fold(y), fold(z)
    kinetic = 4.0 * (x * x + y * y + z * z) / (length * length)
    slot = slot_ref[...]
    high = jnp.floor((slot + 0.5) * (1.0 / LANES))
    low = slot - high * LANES
    for tile in range(waves // LANES):
        span = slice(tile * LANES, (tile + 1) * LANES)
        at_high = where_bf16(iota((chunks, LANES), 0) == high[:, span], 1.0)
        rows = dot(turned, at_high)
        mine = iota((LANES, LANES), 0) == low[:, span]
        re = jnp.sum(jnp.where(mine, rows[:LANES], 0.0), axis=0, keepdims=True)
        im = jnp.sum(jnp.where(mine, rows[LANES:], 0.0), axis=0, keepdims=True)
        both = jnp.concatenate([re, im], axis=0)
        psi = psi_ref[:, span].astype(jnp.float32)
        hpsi_ref[:, span] = (both + kinetic[:, span] * psi + added[0:2, span]).astype(jnp.bfloat16)
        spsi_ref[:, span] = (psi + added[2:4, span]).astype(jnp.bfloat16)


def finish(parts, slot, index, psi, beta, atoms, length, planes, chunks, bands):
    blocks = len(parts)
    return pl.pallas_call(
        functools.partial(finish_kernel, length, planes, chunks, blocks, bands),
        out_shape=(
            jax.ShapeDtypeStruct(psi.shape, jnp.bfloat16),
            jax.ShapeDtypeStruct(psi.shape, jnp.bfloat16),
            jax.ShapeDtypeStruct((2, bands), jnp.float32),
        ),
        compiler_params=pltpu.CompilerParams(vmem_limit_bytes=16 * MIB),
        cost_estimate=cost(2.1),
        name="finish",
    )(*parts, slot, index, psi, beta, atoms)


def swap(value, axis, step):
    size = lax.axis_size(axis)
    return lax.ppermute(value, axis, [(k, k ^ step) for k in range(size)])


def doubles(size):
    return size & (size - 1) == 0


def doubling_steps(size):
    steps = [1 << place for place in range(size.bit_length() - 1)]
    return steps[:1] + steps[:0:-1]


def from_blocks(value, axis):
    size = lax.axis_size(axis)
    found = {0: value}
    step = size // 2
    while step:
        found.update({s + step: swap(found[s], axis, step) for s in list(found)})
        step //= 2
    return [found[s] for s in range(size)]


def from_bands(value, axis, after):
    size = lax.axis_size(axis)
    if not doubles(size):
        pairs = [[(k, (k + s) % size) for k in range(size)] for s in range(1, size)]
        held = [value] + [lax.ppermute(value, axis, pair) for pair in pairs]
        return [part[:, None] for part in held]
    held = [value[:, None]]
    for step in doubling_steps(size):
        if len(held) == 1:
            other = swap(value, axis, step)
            other, _ = lax.optimization_barrier((other, after))
            held.append(other[:, None])
        else:
            joined = jnp.concatenate(held, axis=1)
            held = [joined, swap(joined, axis, step)]
    return held


def atom_blocks(matrix):
    atoms, each = matrix.shape[0], matrix.shape[1]
    same = jnp.eye(atoms, dtype=matrix.dtype)[:, None, :, None]
    square = (same * jnp.transpose(matrix, (0, 2, 1))[:, :, None, :]).reshape(atoms * each, atoms * each)
    return jnp.pad(square, ((0, LANES - atoms * each), (0, LANES - atoms * each)))


def on_device(psi, gvec_index, vloc, beta, dmat, qmat):
    length = vloc.shape[0]
    planes = vloc.shape[1]
    width = psi.shape[2]
    blocks = lax.axis_size("pw")
    bands = lax.axis_size("band")
    chunks = round_up(width // LANES + planes, 16)
    index = gvec_index.reshape(1, width)
    mine = psi.reshape(2, width)
    pay, slot = group_waves(index, mine, length, planes, chunks)
    pays = from_blocks(pay, "pw")
    sums = project(from_bands(mine, "band", pay), beta, bands)
    outs = lattice(pays, sums, vloc, length, planes, chunks)
    dmat, qmat, _ = lax.optimization_barrier((dmat, qmat, outs[0]))
    atoms = jnp.concatenate([atom_blocks(dmat), atom_blocks(qmat)], axis=1)
    parts = [outs[0]] + [swap(outs[s], "pw", s) for s in range(1, blocks)]
    hpsi, spsi, gram = finish(parts, slot, index, mine, beta, atoms, length, planes, chunks, bands)
    return (hpsi.reshape(2, 1, width), spsi.reshape(2, 1, width), gram.reshape(2, 1, bands))


def solution(mesh):
    in_specs = (P(None, "band", "pw"), P("pw"), P(None, "pw", None), P(None, None, "pw"), P(), P())
    out_specs = (P(None, "band", "pw"), P(None, "band", "pw"), P(None, "band", None))
    return jax.shard_map(
        on_device, mesh=mesh, in_specs=in_specs, out_specs=out_specs, check_vma=False
    )
```

```python
import functools

import jax
import jax.numpy as jnp
import ml_dtypes
import numpy as np
from jax import lax
from jax.experimental import pallas as pl
from jax.experimental.pallas import tpu as pltpu
from jax.sharding import PartitionSpec as P

LANES = 128
MIB = 1024 * 1024


def cost(us):
    return pl.CostEstimate(flops=int(us * 1e9), bytes_accessed=MIB, transcendentals=0)


def round_up(value, unit):
    return -(-value // unit) * unit


def dft_parts(length):
    counter = np.arange(length)
    phase = counter[:, None] * counter[None, :] % length
    angle = phase.astype(np.float32) * np.float32(2.0 * np.pi / length)
    factor = np.float32(1.0) / np.sqrt(np.float32(length))
    return (np.cos(angle) * factor).astype(np.float32), (np.sin(angle) * factor).astype(np.float32)


def as_bf16(array):
    return np.asarray(array).astype(ml_dtypes.bfloat16)


def tables_of(length, planes, blocks):
    half = length // 2
    cosine, sine = dft_parts(length)
    rows = round_up(planes, 8)
    own = np.zeros((blocks, 2 * rows, length), np.float32)
    for block in range(blocks):
        span = slice(block * planes, (block + 1) * planes)
        own[block, :planes] = cosine[span]
        own[block, rows : rows + planes] = sine[span]
    def square(c, s, size):
        pad = ((0, size - half), (0, size - half))
        c, s = np.pad(c, pad), np.pad(s, pad)
        return np.block([[c, -s], [s, c]])

    first = slice(0, half)
    even, odd = slice(0, None, 2), slice(1, None, 2)
    along_z = np.stack(
        [
            square(cosine[even, first], -sine[even, first], LANES),
            square(cosine[odd, first], -sine[odd, first], LANES),
            square(cosine[first, even], sine[first, even], LANES),
            square(cosine[first, odd], sine[first, odd], LANES),
        ]
    )
    along_x = np.stack(
        [
            square(cosine[first, even], sine[first, even], half),
            square(cosine[first, odd], sine[first, odd], half),
            square(cosine[even, first], -sine[even, first], half),
            square(cosine[odd, first], -sine[odd, first], half),
        ]
    )
    pieces = [along_z, along_x, own]
    pieces = [np.pad(piece, ((0, 0), (0, 0), (0, 2 * LANES - piece.shape[2]))) for piece in pieces]
    return as_bf16(np.concatenate([piece.reshape(-1, 2 * LANES) for piece in pieces]))


def cell_parts(index, length):
    cell = index.astype(jnp.float32)
    x = jnp.floor((cell + 0.5) * (1.0 / (length * length)))
    rest = cell - x * (length * length)
    y = jnp.floor((rest + 0.5) * (1.0 / length))
    return x, y, rest - y * length


def iota(shape, dim):
    return lax.broadcasted_iota(jnp.int32, shape, dim).astype(jnp.float32)


def where_bf16(mask, value):
    return jnp.where(mask, value, 0.0).astype(jnp.bfloat16)


def dot(left, right):
    return jnp.dot(left, right, preferred_element_type=jnp.float32)


def dot_lanes(left, right):
    return lax.dot_general(left, right, (((1,), (1,)), ((), ())), preferred_element_type=jnp.float32)


def fetch_all(pairs, sems):
    copies = [pltpu.make_async_copy(source, target, sems.at[n]) for n, (source, target) in enumerate(pairs)]
    for copy in copies:
        copy.start()
    return copies


def group_kernel(
    length, planes, chunks, gvec_hbm, psi_hbm, pay_ref, slot_ref, hot, counts, spread, pick, gvec_ref, psi_ref, sems
):
    for copy in fetch_all(((gvec_hbm, gvec_ref), (psi_hbm, psi_ref)), sems):
        copy.wait()
    waves = gvec_ref.shape[1]
    tiles = waves // LANES
    rows = round_up(planes, 16)
    x, y, z = cell_parts(gvec_ref[...], length)
    z_half = jnp.floor(z * 0.5)
    z = z_half + (z - 2.0 * z_half) * LANES
    psi = psi_ref[...].astype(jnp.float32)
    plane = iota((rows, LANES), 0)
    for tile in range(tiles):
        span = slice(tile * LANES, (tile + 1) * LANES)
        hot[tile * rows : (tile + 1) * rows, :] = where_bf16(plane == x[:, span], 1.0)
    upto = jnp.where(iota((LANES, LANES), 0) <= iota((LANES, LANES), 1), 1.0, 0.0)
    upto = jnp.concatenate([upto, jnp.ones((LANES, LANES), jnp.float32)], axis=1)
    counts[...] = dot(hot[...], upto.astype(jnp.bfloat16))
    total = jnp.zeros((rows, LANES), jnp.float32)
    for tile in range(tiles):
        total = total + counts[tile * rows : (tile + 1) * rows, LANES:]
    need = jnp.maximum(jnp.floor((total + (LANES - 0.5)) * (1.0 / LANES)), 1.0)
    need = jnp.where(plane < planes, need, 0.0)
    below = where_bf16(iota((rows, rows), 1) < iota((rows, rows), 0), 1.0)
    first = dot(below, need.astype(jnp.bfloat16))
    ends = jnp.where((plane < planes) & (iota((rows, LANES), 1) >= first + need), 1.0, 0.0)
    chunk_plane = jnp.sum(ends, axis=0, keepdims=True)
    running = first * LANES - 1.0
    upper = iota((chunks, LANES), 0)
    lower = iota((LANES, LANES), 0)
    for tile in range(tiles):
        span = slice(tile * LANES, (tile + 1) * LANES)
        part = slice(tile * rows, (tile + 1) * rows)
        mine = plane == x[:, span]
        slot = jnp.where(mine, counts[part, :LANES] + running, 0.0)
        slot = jnp.sum(slot, axis=0, keepdims=True)
        running = running + counts[part, LANES:]
        slot_ref[:, span] = slot
        high = jnp.floor((slot + 0.5) * (1.0 / LANES))
        at_high = upper == high
        spread[0:chunks, span] = where_bf16(at_high, psi[0:1, span])
        spread[chunks : 2 * chunks, span] = where_bf16(at_high, psi[1:2, span])
        spread[2 * chunks : 3 * chunks, span] = where_bf16(at_high, y[:, span])
        spread[3 * chunks : 4 * chunks, span] = where_bf16(at_high, z[:, span])
        pick[:, span] = where_bf16(lower == slot - high * LANES, 1.0)
    pay_ref[0 : 4 * chunks, :] = dot_lanes(spread[...], pick[...]).astype(jnp.bfloat16)
    used = jnp.sum(need, axis=0, keepdims=True)
    pay_ref[4 * chunks :, :] = jnp.where(iota((16, LANES), 0) == 0.0, chunk_plane, used).astype(jnp.bfloat16)


def group_waves(index, psi, length, planes, chunks):
    waves = index.shape[1]
    rows = round_up(planes, 16)
    tiles = waves // LANES
    return pl.pallas_call(
        functools.partial(group_kernel, length, planes, chunks),
        out_shape=(
            jax.ShapeDtypeStruct((4 * chunks + 16, LANES), jnp.bfloat16),
            jax.ShapeDtypeStruct((1, waves), jnp.float32),
        ),
        scratch_shapes=[
            pltpu.VMEM((tiles * rows, LANES), jnp.bfloat16),
            pltpu.VMEM((tiles * rows, 2 * LANES), jnp.float32),
            pltpu.VMEM((4 * chunks, waves), jnp.bfloat16),
            pltpu.VMEM((LANES, waves), jnp.bfloat16),
            pltpu.VMEM((1, waves), jnp.int32),
            pltpu.VMEM((2, waves), jnp.bfloat16),
            pltpu.SemaphoreType.DMA((2,)),
        ],
        in_specs=[pl.BlockSpec(memory_space=pl.ANY)] * 2,
        compiler_params=pltpu.CompilerParams(vmem_limit_bytes=24 * MIB),
        cost_estimate=cost(3.4),
        name="group_waves",
    )(index, psi)


def lattice_kernel(length, planes, chunks, blocks, *refs):
    pays = refs[:blocks]
    sums_ref, vloc_hbm, tables = refs[blocks : blocks + 3]
    outs = refs[blocks + 3 : 2 * blocks + 3]
    wide, cells_e, cells_o, phases, vloc, result, maps, maps_s, sems, vloc_sem = refs[2 * blocks + 3 :]
    half = length // 2
    rows = round_up(planes, 8)
    both = 2 * rows
    pitch = both + 1
    spare = blocks * planes
    me = lax.axis_index("pw")
    for s in range(blocks):
        maps[s * 8 : (s + 1) * 8, :] = pays[s][4 * chunks : 4 * chunks + 16, :].astype(jnp.int32)[:8]
    (fetch,) = fetch_all(((maps, maps_s),), sems)

    def load(k, _):
        pltpu.make_async_copy(vloc_hbm.at[:, k, :], vloc.at[k], vloc_sem).start()
        return 0

    lax.fori_loop(0, planes, load, 0)
    for s in range(blocks):
        wide[s * 4 * chunks : (s + 1) * 4 * chunks, :] = pays[s][0 : 4 * chunks, :].astype(jnp.float32)
    own_at = 8 * LANES + 4 * length + pl.multiple_of(me * both, 16)
    own = tables[pl.ds(own_at, both), :][:, :length]

    def along_z(n):
        return tables[2 * LANES * n : 2 * LANES * (n + 1), :]

    def along_x(n):
        return tables[8 * LANES + length * n : 8 * LANES + length * (n + 1), :][:, :length]

    fetch.wait()
    used = maps_s[1, 0]
    for s in range(1, blocks):
        used = jnp.maximum(used, maps_s[s * 8 + 1, 0])
    level = iota((2 * LANES, LANES), 0)
    level_y = level[:length]
    group = 4 if blocks % 4 == 0 else 1
    ahead = 8 if blocks == group else 1
    batch = 16 if planes % 16 == 0 else 1
    turns = (used + ahead - 1) // ahead

    def place(s, c):
        at = maps_s[s * 8, c]
        x = (me ^ s) * planes + at
        return jnp.where(at < planes, x // 2 + x % 2 * half, spare)

    def row(s, part, c):
        return wide[pl.ds((s * 4 + part) * chunks + c, 1), :]

    def items(turn, base):
        return [(s, turn * ahead + j) for s in range(base, base + group) for j in range(ahead)]

    def pick_z(s, c):
        return where_bf16(level == row(s, 3, c), 1.0)

    def phases_of(todo):
        wanted = [where_bf16(level_y == row(s, 2, c), 1.0) for s, c in todo]
        found = []
        for n in range(0, len(todo), 2):
            both_phases = dot(own, jnp.concatenate(wanted[n : n + 2], axis=1))
            found += [both_phases[:, :LANES], both_phases[:, LANES:]][: len(wanted[n : n + 2])]
        return found

    def forward(turn, _):
        for base in range(0, blocks, group):
            todo = items(turn, base)
            found = phases_of(todo)
            mixed = []
            for (s, c), phase in zip(todo, found):
                phases[s * chunks + c] = phase.astype(jnp.bfloat16)
                re, im = row(s, 0, c), row(s, 1, c)
                cos, sin = phase[:rows], phase[rows:]
                both_parts = jnp.concatenate([re * cos - im * sin, re * sin + im * cos], axis=0)
                mixed.append(both_parts.astype(jnp.bfloat16))
            found = [dot_lanes(value, pick_z(s, c)) for (s, c), value in zip(todo, mixed)]
            spans = [place(s, c) for s, c in todo]
            for n, (s, c) in enumerate(todo):
                span = pl.ds(spans[n] * pitch, both)
                if n % ahead == 0:
                    fresh = (c == 0) | (spans[n] != place(s, jnp.maximum(c - 1, 0)))
                    before_e, before_o = cells_e[span, :], cells_o[span, :]
                else:
                    fresh = spans[n] != spans[n - 1]
                    before_e, before_o = part_e, part_o
                part_e = found[n][:, :LANES] + jnp.where(fresh, 0.0, before_e)
                part_o = found[n][:, LANES:] + jnp.where(fresh, 0.0, before_o)
                cells_e[span, :] = part_e
                cells_o[span, :] = part_o
        return 0

    lax.fori_loop(0, turns, forward, 0)
    pltpu.make_async_copy(vloc, vloc, vloc_sem).wait()

    def strided(start):
        return pl.ds(start, half, stride=pitch)

    def beside(left, right):
        return jnp.concatenate([left, right], axis=1)

    def above(upper, lower):
        return jnp.concatenate([upper, lower], axis=0)

    def middle(turn, _):
        many = [turn * batch + j for j in range(batch)]
        starts = [k + odd * half * pitch for k in many for odd in range(2)]

        def pull(cells):
            return jnp.concatenate(
                [
                    beside(cells[strided(at), :], cells[strided(at + rows), :]).astype(jnp.bfloat16)
                    for at in starts
                ],
                axis=0,
            )

        even = dot(pull(cells_e), along_z(0))
        odd = dot(pull(cells_o), along_z(1))
        low, high = (even + odd).astype(jnp.bfloat16), (even - odd).astype(jnp.bfloat16)

        def stacked(n):
            part = slice(n * half, (n + 1) * half)
            return above(
                beside(low[part, :LANES], high[part, :LANES]),
                beside(low[part, LANES:], high[part, LANES:]),
            )

        sums, differences = [], []
        for j, k in enumerate(many):
            even = dot(along_x(0), stacked(2 * j))
            odd = dot(along_x(1), stacked(2 * j + 1))
            field = vloc[k]
            field = beside(field[:, :LANES], beside(field[:, half:], field[:, : LANES - half]))
            near, far = field[:half], field[half:]
            first = (even + odd) * above(near, near)
            second = (even - odd) * above(far, far)
            for table, value in ((along_x(2), first + second), (along_x(3), first - second)):
                back = dot(table, value.astype(jnp.bfloat16))
                total, change = back[:, :LANES] + back[:, LANES:], back[:, :LANES] - back[:, LANES:]
                sums.append(beside(total[:half], total[half:]).astype(jnp.bfloat16))
                differences.append(beside(change[:half], change[half:]).astype(jnp.bfloat16))
        even = dot(jnp.concatenate(sums, axis=0), along_z(2))
        odd = dot(jnp.concatenate(differences, axis=0), along_z(3))
        for n, at in enumerate(starts):
            part = slice(n * half, (n + 1) * half)
            cells_e[strided(at), :] = even[part, :LANES]
            cells_e[strided(at + rows), :] = even[part, LANES:]
            cells_o[strided(at), :] = odd[part, :LANES]
            cells_o[strided(at + rows), :] = odd[part, LANES:]
        return 0

    lax.fori_loop(0, planes // batch, middle, 0)

    def backward(turn, _):
        for base in range(0, blocks, group):
            todo = items(turn, base)
            found = []
            for s, c in todo:
                span = pl.ds(place(s, c) * pitch, both)
                value = beside(cells_e[span, :], cells_o[span, :]).astype(jnp.bfloat16)
                found.append(dot(value, pick_z(s, c)))
            for (s, c), part in zip(todo, found):
                phase = phases[s * chunks + c].astype(jnp.float32)
                re, im = part[:rows], part[rows:]
                cos, sin = phase[:rows], phase[rows:]
                result[pl.ds(s * 2 * chunks + c, 1), :] = jnp.sum(re * cos + im * sin, axis=0, keepdims=True)
                result[pl.ds((s * 2 + 1) * chunks + c, 1), :] = jnp.sum(im * cos - re * sin, axis=0, keepdims=True)
        return 0

    spare_span = pl.ds(spare * pitch, both)
    cells_e[spare_span, :] = jnp.zeros((both, LANES), jnp.float32)
    cells_o[spare_span, :] = jnp.zeros((both, LANES), jnp.float32)
    result[...] = jnp.zeros_like(result)
    lax.fori_loop(0, turns, backward, 0)
    rest = sums_ref[...]
    pieces = []
    for _ in range(3):
        pieces.append(rest.astype(jnp.bfloat16))
        rest = rest - pieces[-1].astype(jnp.float32)
    size = sums_ref.shape[0]
    for s in range(blocks):
        outs[s][0 : 2 * chunks, :] = result[s * 2 * chunks : (s + 1) * 2 * chunks, :].astype(jnp.bfloat16)
        for n, piece in enumerate(pieces):
            outs[s][2 * chunks + n * size : 2 * chunks + (n + 1) * size, :] = piece


def lattice(pays, sums, vloc, length, planes, chunks):
    blocks = len(pays)
    rows = round_up(planes, 8)
    tables = tables_of(length, planes, blocks)
    vmem = pl.BlockSpec(memory_space=pltpu.VMEM)
    return pl.pallas_call(
        functools.partial(lattice_kernel, length, planes, chunks, blocks),
        out_shape=[jax.ShapeDtypeStruct((2 * chunks + 3 * sums.shape[0], LANES), jnp.bfloat16)] * blocks,
        in_specs=[vmem] * (blocks + 1) + [pl.BlockSpec(memory_space=pl.ANY), vmem],
        out_specs=[vmem] * blocks,
        scratch_shapes=[
            pltpu.VMEM((blocks * 4 * chunks, LANES), jnp.float32),
            pltpu.VMEM((round_up((blocks * planes + 1) * (2 * rows + 1), 8), LANES), jnp.float32),
            pltpu.VMEM((round_up((blocks * planes + 1) * (2 * rows + 1), 8), LANES), jnp.float32),
            pltpu.VMEM((blocks * chunks, 2 * rows, LANES), jnp.bfloat16),
            pltpu.VMEM((planes, length, length), jnp.float32),
            pltpu.VMEM((blocks * 2 * chunks, LANES), jnp.float32),
            pltpu.VMEM((blocks * 8, LANES), jnp.int32),
            pltpu.SMEM((blocks * 8, LANES), jnp.int32),
            pltpu.SemaphoreType.DMA((1,)),
            pltpu.SemaphoreType.DMA,
        ],
        compiler_params=pltpu.CompilerParams(vmem_limit_bytes=48 * MIB),
        cost_estimate=cost(36.0),
        name="lattice",
    )(*pays, sums, vloc, tables)


def project_kernel(bands, *refs):
    beta_hbm, out_ref, beta_ref, sems = refs[-4:]
    (fetch,) = fetch_all(((beta_hbm, beta_ref),), sems)
    every = [ref[...].astype(jnp.float32) for ref in refs[:-4]]
    count = beta_ref.shape[1]
    rows = out_ref.shape[0] // 2
    pad = [jnp.zeros((rows - bands, every[0].shape[2]), jnp.float32)] if rows > bands else []
    re = jnp.concatenate([value[0] for value in every] + pad, axis=0)
    im = jnp.concatenate([value[1] for value in every] + pad, axis=0)
    fetch.wait()
    stack = jnp.concatenate([re, im], axis=0).astype(jnp.bfloat16)
    on_re, on_im = dot_lanes(beta_ref[0], stack), dot_lanes(beta_ref[1], stack)
    found = jnp.concatenate([on_re[:, :rows] + on_im[:, rows:], on_re[:, rows:] - on_im[:, :rows]], axis=1)
    out_ref[...] = jnp.zeros_like(out_ref)
    out_ref[:, :count] = found.T
    own_re, own_im = re[:1], im[:1]
    over = jnp.concatenate(
        [
            jnp.sum(re * own_re + im * own_im, axis=1, keepdims=True),
            jnp.sum(im * own_re - re * own_im, axis=1, keepdims=True),
        ],
        axis=0,
    )
    out_ref[...] = jnp.where(iota(out_ref.shape, 1) == count, over, out_ref[...])


def project(every, beta, bands):
    return pl.pallas_call(
        functools.partial(project_kernel, bands),
        out_shape=jax.ShapeDtypeStruct((2 * round_up(bands, 8), LANES), jnp.float32),
        in_specs=[pl.BlockSpec(memory_space=pltpu.VMEM)] * len(every) + [pl.BlockSpec(memory_space=pl.ANY)],
        scratch_shapes=[pltpu.VMEM(beta.shape, beta.dtype), pltpu.SemaphoreType.DMA((1,))],
        compiler_params=pltpu.CompilerParams(vmem_limit_bytes=16 * MIB),
        cost_estimate=cost(1.2),
        name="project",
    )(*every, beta)


def finish_kernel(length, planes, chunks, blocks, *refs):
    parts = refs[:blocks]
    slot_ref, gvec_ref, psi_ref, beta_ref, atoms_ref, hpsi_ref, spsi_ref = refs[blocks:]
    waves = slot_ref.shape[1]
    count = beta_ref.shape[1]
    total = parts[0][...].astype(jnp.float32)
    for part in parts[1:]:
        total = total + part[...].astype(jnp.float32)
    size = (total.shape[0] - 2 * chunks) // 3
    half_size = size // 2
    sums = [total[2 * chunks + n * size : 2 * chunks + (n + 1) * size] for n in range(3)]
    sums = sums[0] + (sums[1] + sums[2])
    coef = jnp.dot(sums, atoms_ref[...], precision=lax.Precision.HIGHEST, preferred_element_type=jnp.float32)
    coef = coef.astype(jnp.bfloat16).astype(jnp.float32)
    d_re, d_im = coef[:1, :count], coef[half_size : half_size + 1, :count]
    q_re, q_im = coef[:1, LANES : LANES + count], coef[half_size : half_size + 1, LANES : LANES + count]
    none = jnp.zeros((4, count), jnp.float32)
    on_re = jnp.concatenate([d_re, d_im, q_re, q_im, none], axis=0).astype(jnp.bfloat16)
    on_im = jnp.concatenate([-d_im, d_re, -q_im, q_re, none], axis=0).astype(jnp.bfloat16)
    added = dot(on_re, beta_ref[0]) + dot(on_im, beta_ref[1])

    local = total[: 2 * chunks]
    turned = jnp.concatenate([local[:chunks].T, local[chunks:].T], axis=0).astype(jnp.bfloat16)
    x, y, z = cell_parts(gvec_ref[...], length)
    x = x + (lax.axis_index("pw") * planes).astype(jnp.float32)

    def fold(level):
        return jnp.where(level < length // 2, level, level - length)

    x, y, z = fold(x), fold(y), fold(z)
    kinetic = 4.0 * (x * x + y * y + z * z) / (length * length)
    slot = slot_ref[...]
    high = jnp.floor((slot + 0.5) * (1.0 / LANES))
    low = slot - high * LANES
    for tile in range(waves // LANES):
        span = slice(tile * LANES, (tile + 1) * LANES)
        at_high = where_bf16(iota((chunks, LANES), 0) == high[:, span], 1.0)
        rows = dot(turned, at_high)
        mine = iota((LANES, LANES), 0) == low[:, span]
        re = jnp.sum(jnp.where(mine, rows[:LANES], 0.0), axis=0, keepdims=True)
        im = jnp.sum(jnp.where(mine, rows[LANES:], 0.0), axis=0, keepdims=True)
        both = jnp.concatenate([re, im], axis=0)
        psi = psi_ref[:, span].astype(jnp.float32)
        hpsi_ref[:, span] = (both + kinetic[:, span] * psi + added[0:2, span]).astype(jnp.bfloat16)
        spsi_ref[:, span] = (psi + added[2:4, span]).astype(jnp.bfloat16)


def finish(parts, slot, index, psi, beta, atoms, length, planes, chunks):
    blocks = len(parts)
    return pl.pallas_call(
        functools.partial(finish_kernel, length, planes, chunks, blocks),
        out_shape=(
            jax.ShapeDtypeStruct(psi.shape, jnp.bfloat16),
            jax.ShapeDtypeStruct(psi.shape, jnp.bfloat16),
        ),
        compiler_params=pltpu.CompilerParams(vmem_limit_bytes=16 * MIB),
        cost_estimate=cost(2.1),
        name="finish",
    )(*parts, slot, index, psi, beta, atoms)


def gram_kernel(waves, bands, count, *refs):
    atoms_ref, gram_ref = refs[-2:]
    sums = refs[0][...]
    for ref in refs[1:-2]:
        sums = sums + ref[...]
    half_size = sums.shape[0] // 2
    coef = jnp.dot(sums, atoms_ref[...], precision=lax.Precision.HIGHEST, preferred_element_type=jnp.float32)
    coef = coef.astype(jnp.bfloat16).astype(jnp.float32)
    own_re, own_im = sums[:1], sums[half_size : half_size + 1]
    each_re, each_im = coef[:half_size, LANES:], coef[half_size:, LANES:]
    over = iota((half_size, LANES), 1) == count
    gram_re = own_re * each_re + own_im * each_im + jnp.where(over, sums[:half_size], 0.0)
    gram_im = own_re * each_im - own_im * each_re + jnp.where(over, sums[half_size:], 0.0)
    slot_at = lax.broadcasted_iota(jnp.int32, (half_size, bands), 0)
    if doubles(bands):
        turn = lax.axis_index("band")
        for place, step in enumerate(doubling_steps(bands)):
            turn = turn ^ (((slot_at >> place) & 1) * step)
    else:
        turn = lax.axis_index("band") - slot_at
        turn = jnp.where(turn < 0, turn + bands, turn)
    here = turn == lax.broadcasted_iota(jnp.int32, (half_size, bands), 1)
    here = here & (lax.broadcasted_iota(jnp.int32, (half_size, bands), 0) < bands)
    for n, value in enumerate((gram_re, gram_im)):
        value = jnp.sum(value, axis=1, keepdims=True)
        value = jnp.sum(jnp.where(here, value, 0.0), axis=0, keepdims=True)
        gram_ref[n : n + 1, :] = value * (1.0 / (waves))


def gram_row(parts, atoms, waves, bands, count):
    return pl.pallas_call(
        functools.partial(gram_kernel, waves, bands, count),
        out_shape=jax.ShapeDtypeStruct((2, bands), jnp.float32),
        compiler_params=pltpu.CompilerParams(vmem_limit_bytes=16 * MIB),
        cost_estimate=cost(0.7),
        name="gram_row",
    )(*parts, atoms)


def swap(value, axis, step):
    size = lax.axis_size(axis)
    return lax.ppermute(value, axis, [(k, k ^ step) for k in range(size)])


def doubles(size):
    return size & (size - 1) == 0


def doubling_steps(size):
    steps = [1 << place for place in range(size.bit_length() - 1)]
    return steps[:1] + steps[:0:-1]


def from_blocks(value, axis):
    size = lax.axis_size(axis)
    found = {0: value}
    step = size // 2
    while step:
        found.update({s + step: swap(found[s], axis, step) for s in list(found)})
        step //= 2
    return [found[s] for s in range(size)]


def from_bands_early(value, axis, after):
    size = lax.axis_size(axis)
    if not doubles(size):
        pairs = [[(k, (k + s) % size) for k in range(size)] for s in range(1, size)]
        held = [value] + [lax.ppermute(value, axis, pair) for pair in pairs]
        return [part[:, None] for part in held]
    held = [value[:, None]]
    for step in doubling_steps(size)[:-1]:
        if len(held) == 1:
            other = swap(value, axis, step)
            other, _ = lax.optimization_barrier((other, after))
            held.append(other[:, None])
        else:
            joined = jnp.concatenate(held, axis=1)
            held = [joined, swap(joined, axis, step)]
    return held


def from_bands_late(held, axis):
    size = lax.axis_size(axis)
    if size == 1 or not doubles(size):
        return held
    joined = jnp.concatenate(held, axis=1)
    return [joined, swap(joined, axis, doubling_steps(size)[-1])]


def atom_blocks(matrix):
    atoms, each = matrix.shape[0], matrix.shape[1]
    same = jnp.eye(atoms, dtype=matrix.dtype)[:, None, :, None]
    square = (same * jnp.transpose(matrix, (0, 2, 1))[:, :, None, :]).reshape(atoms * each, atoms * each)
    return jnp.pad(square, ((0, LANES - atoms * each), (0, LANES - atoms * each)))


def on_device(psi, gvec_index, vloc, beta, dmat, qmat):
    length = vloc.shape[0]
    planes = vloc.shape[1]
    width = psi.shape[2]
    blocks = lax.axis_size("pw")
    bands = lax.axis_size("band")
    chunks = round_up(width // LANES + planes, 16)
    index = gvec_index.reshape(1, width)
    mine = psi.reshape(2, width)
    pay, slot = group_waves(index, mine, length, planes, chunks)
    pays = from_blocks(pay, "pw")
    early = from_bands_early(mine, "band", pay)
    later, _ = lax.optimization_barrier((mine, pay))
    outs = lattice(pays, project([later[:, None]], beta, 1), vloc, length, planes, chunks)
    parts = [outs[0]] + [swap(outs[s], "pw", s) for s in range(1, blocks)]
    dmat, qmat, early, _ = lax.optimization_barrier((dmat, qmat, early, outs[0]))
    every = from_bands_late(early, "band")
    atoms = jnp.concatenate([atom_blocks(dmat), atom_blocks(qmat)], axis=1)
    hpsi, spsi = finish(parts, slot, index, mine, beta, atoms, length, planes, chunks)
    sums = project(every, beta, bands)
    sums = [sums] + [swap(sums, "pw", s) for s in range(1, blocks)]
    gram = gram_row(sums, atoms, width * blocks, bands, beta.shape[1])
    return (hpsi.reshape(2, 1, width), spsi.reshape(2, 1, width), gram.reshape(2, 1, bands))


def solution(mesh):
    in_specs = (P(None, "band", "pw"), P("pw"), P(None, "pw", None), P(None, None, "pw"), P(), P())
    out_specs = (P(None, "band", "pw"), P(None, "band", "pw"), P(None, "band", None))
    return jax.shard_map(
        on_device, mesh=mesh, in_specs=in_specs, out_specs=out_specs, check_vma=False
    )
```

```python
import functools

import jax
import jax.numpy as jnp
import ml_dtypes
import numpy as np
from jax import lax
from jax.experimental import pallas as pl
from jax.experimental.pallas import tpu as pltpu
from jax.sharding import PartitionSpec as P

LANES = 128
MIB = 1024 * 1024


def cost(us):
    return pl.CostEstimate(flops=int(us * 1e9), bytes_accessed=MIB, transcendentals=0)


def round_up(value, unit):
    return -(-value // unit) * unit


def dft_parts(length):
    counter = np.arange(length)
    phase = counter[:, None] * counter[None, :] % length
    angle = phase.astype(np.float32) * np.float32(2.0 * np.pi / length)
    factor = np.float32(1.0) / np.sqrt(np.float32(length))
    return (np.cos(angle) * factor).astype(np.float32), (np.sin(angle) * factor).astype(np.float32)


def as_bf16(array):
    return np.asarray(array).astype(ml_dtypes.bfloat16)


def tables_of(length, planes, blocks):
    half = length // 2
    cosine, sine = dft_parts(length)
    rows = round_up(planes, 8)
    own = np.zeros((blocks, 2 * rows, length), np.float32)
    for block in range(blocks):
        span = slice(block * planes, (block + 1) * planes)
        own[block, :planes] = cosine[span]
        own[block, rows : rows + planes] = sine[span]
    def square(c, s, size):
        pad = ((0, size - half), (0, size - half))
        c, s = np.pad(c, pad), np.pad(s, pad)
        return np.block([[c, -s], [s, c]])

    first = slice(0, half)
    even, odd = slice(0, None, 2), slice(1, None, 2)
    along_z = np.stack(
        [
            square(cosine[even, first], -sine[even, first], LANES),
            square(cosine[odd, first], -sine[odd, first], LANES),
            square(cosine[first, even], sine[first, even], LANES),
            square(cosine[first, odd], sine[first, odd], LANES),
        ]
    )
    along_x = np.stack(
        [
            square(cosine[first, even], sine[first, even], half),
            square(cosine[first, odd], sine[first, odd], half),
            square(cosine[even, first], -sine[even, first], half),
            square(cosine[odd, first], -sine[odd, first], half),
        ]
    )
    pieces = [along_z, along_x, own]
    pieces = [np.pad(piece, ((0, 0), (0, 0), (0, 2 * LANES - piece.shape[2]))) for piece in pieces]
    return as_bf16(np.concatenate([piece.reshape(-1, 2 * LANES) for piece in pieces]))


def cell_parts(index, length):
    cell = index.astype(jnp.float32)
    x = jnp.floor((cell + 0.5) * (1.0 / (length * length)))
    rest = cell - x * (length * length)
    y = jnp.floor((rest + 0.5) * (1.0 / length))
    return x, y, rest - y * length


def iota(shape, dim):
    return lax.broadcasted_iota(jnp.int32, shape, dim).astype(jnp.float32)


def where_bf16(mask, value):
    return jnp.where(mask, value, 0.0).astype(jnp.bfloat16)


def dot(left, right):
    return jnp.dot(left, right, preferred_element_type=jnp.float32)


def dot_lanes(left, right):
    return lax.dot_general(left, right, (((1,), (1,)), ((), ())), preferred_element_type=jnp.float32)


def fetch_all(pairs, sems):
    copies = [pltpu.make_async_copy(source, target, sems.at[n]) for n, (source, target) in enumerate(pairs)]
    for copy in copies:
        copy.start()
    return copies


def group_kernel(
    length, planes, chunks, gvec_hbm, psi_hbm, pay_ref, slot_ref, hot, counts, spread, pick, gvec_ref, psi_ref, sems
):
    for copy in fetch_all(((gvec_hbm, gvec_ref), (psi_hbm, psi_ref)), sems):
        copy.wait()
    waves = gvec_ref.shape[1]
    tiles = waves // LANES
    rows = round_up(planes, 16)
    x, y, z = cell_parts(gvec_ref[...], length)
    z_half = jnp.floor(z * 0.5)
    z = z_half + (z - 2.0 * z_half) * LANES
    psi = psi_ref[...].astype(jnp.float32)
    plane = iota((rows, LANES), 0)
    for tile in range(tiles):
        span = slice(tile * LANES, (tile + 1) * LANES)
        hot[tile * rows : (tile + 1) * rows, :] = where_bf16(plane == x[:, span], 1.0)
    upto = jnp.where(iota((LANES, LANES), 0) <= iota((LANES, LANES), 1), 1.0, 0.0)
    upto = jnp.concatenate([upto, jnp.ones((LANES, LANES), jnp.float32)], axis=1)
    counts[...] = dot(hot[...], upto.astype(jnp.bfloat16))
    total = jnp.zeros((rows, LANES), jnp.float32)
    for tile in range(tiles):
        total = total + counts[tile * rows : (tile + 1) * rows, LANES:]
    need = jnp.maximum(jnp.floor((total + (LANES - 0.5)) * (1.0 / LANES)), 1.0)
    need = jnp.where(plane < planes, need, 0.0)
    below = where_bf16(iota((rows, rows), 1) < iota((rows, rows), 0), 1.0)
    first = dot(below, need.astype(jnp.bfloat16))
    ends = jnp.where((plane < planes) & (iota((rows, LANES), 1) >= first + need), 1.0, 0.0)
    chunk_plane = jnp.sum(ends, axis=0, keepdims=True)
    running = first * LANES - 1.0
    upper = iota((chunks, LANES), 0)
    lower = iota((LANES, LANES), 0)
    for tile in range(tiles):
        span = slice(tile * LANES, (tile + 1) * LANES)
        part = slice(tile * rows, (tile + 1) * rows)
        mine = plane == x[:, span]
        slot = jnp.where(mine, counts[part, :LANES] + running, 0.0)
        slot = jnp.sum(slot, axis=0, keepdims=True)
        running = running + counts[part, LANES:]
        slot_ref[:, span] = slot
        high = jnp.floor((slot + 0.5) * (1.0 / LANES))
        at_high = upper == high
        spread[0:chunks, span] = where_bf16(at_high, psi[0:1, span])
        spread[chunks : 2 * chunks, span] = where_bf16(at_high, psi[1:2, span])
        spread[2 * chunks : 3 * chunks, span] = where_bf16(at_high, y[:, span])
        spread[3 * chunks : 4 * chunks, span] = where_bf16(at_high, z[:, span])
        pick[:, span] = where_bf16(lower == slot - high * LANES, 1.0)
    pay_ref[0 : 4 * chunks, :] = dot_lanes(spread[...], pick[...]).astype(jnp.bfloat16)
    used = jnp.sum(need, axis=0, keepdims=True)
    pay_ref[4 * chunks :, :] = jnp.where(iota((16, LANES), 0) == 0.0, chunk_plane, used).astype(jnp.bfloat16)


def group_waves(index, psi, length, planes, chunks):
    waves = index.shape[1]
    rows = round_up(planes, 16)
    tiles = waves // LANES
    return pl.pallas_call(
        functools.partial(group_kernel, length, planes, chunks),
        out_shape=(
            jax.ShapeDtypeStruct((4 * chunks + 16, LANES), jnp.bfloat16),
            jax.ShapeDtypeStruct((1, waves), jnp.float32),
        ),
        scratch_shapes=[
            pltpu.VMEM((tiles * rows, LANES), jnp.bfloat16),
            pltpu.VMEM((tiles * rows, 2 * LANES), jnp.float32),
            pltpu.VMEM((4 * chunks, waves), jnp.bfloat16),
            pltpu.VMEM((LANES, waves), jnp.bfloat16),
            pltpu.VMEM((1, waves), jnp.int32),
            pltpu.VMEM((2, waves), jnp.bfloat16),
            pltpu.SemaphoreType.DMA((2,)),
        ],
        in_specs=[pl.BlockSpec(memory_space=pl.ANY)] * 2,
        compiler_params=pltpu.CompilerParams(vmem_limit_bytes=24 * MIB),
        cost_estimate=cost(3.4),
        name="group_waves",
    )(index, psi)


def lattice_kernel(length, planes, chunks, blocks, *refs):
    pays = refs[:blocks]
    sums_ref, vloc_hbm, tables = refs[blocks : blocks + 3]
    outs = refs[blocks + 3 : 2 * blocks + 3]
    wide, cells_e, cells_o, phases, vloc, result, maps, maps_s, sems, vloc_sem = refs[2 * blocks + 3 :]
    half = length // 2
    rows = round_up(planes, 8)
    both = 2 * rows
    pitch = both + 1
    spare = blocks * planes
    me = lax.axis_index("pw")
    for s in range(blocks):
        maps[s * 8 : (s + 1) * 8, :] = pays[s][4 * chunks : 4 * chunks + 16, :].astype(jnp.int32)[:8]
    (fetch,) = fetch_all(((maps, maps_s),), sems)

    def load(k, _):
        pltpu.make_async_copy(vloc_hbm.at[:, k, :], vloc.at[k], vloc_sem).start()
        return 0

    lax.fori_loop(0, planes, load, 0)
    for s in range(blocks):
        wide[s * 4 * chunks : (s + 1) * 4 * chunks, :] = pays[s][0 : 4 * chunks, :].astype(jnp.float32)
    own_at = 8 * LANES + 4 * length + pl.multiple_of(me * both, 16)
    own = tables[pl.ds(own_at, both), :][:, :length]

    def along_z(n):
        return tables[2 * LANES * n : 2 * LANES * (n + 1), :]

    def along_x(n):
        return tables[8 * LANES + length * n : 8 * LANES + length * (n + 1), :][:, :length]

    fetch.wait()
    used = maps_s[1, 0]
    for s in range(1, blocks):
        used = jnp.maximum(used, maps_s[s * 8 + 1, 0])
    level = iota((2 * LANES, LANES), 0)
    level_y = level[:length]
    group = 4 if blocks % 4 == 0 else 1
    ahead = 8 if blocks == group else 1
    batch = 24 if planes % 24 == 0 else 1
    turns = (used + ahead - 1) // ahead

    def place(s, c):
        at = maps_s[s * 8, c]
        x = (me ^ s) * planes + at
        return jnp.where(at < planes, x // 2 + x % 2 * half, spare)

    def row(s, part, c):
        return wide[pl.ds((s * 4 + part) * chunks + c, 1), :]

    def items(turn, base):
        return [(s, turn * ahead + j) for s in range(base, base + group) for j in range(ahead)]

    def pick_z(s, c):
        return where_bf16(level == row(s, 3, c), 1.0)

    def phases_of(todo):
        wanted = [where_bf16(level_y == row(s, 2, c), 1.0) for s, c in todo]
        found = []
        for n in range(0, len(todo), 2):
            both_phases = dot(own, jnp.concatenate(wanted[n : n + 2], axis=1))
            found += [both_phases[:, :LANES], both_phases[:, LANES:]][: len(wanted[n : n + 2])]
        return found

    def forward(turn, _):
        for base in range(0, blocks, group):
            todo = items(turn, base)
            found = phases_of(todo)
            mixed = []
            for (s, c), phase in zip(todo, found):
                phases[s * chunks + c] = phase.astype(jnp.bfloat16)
                re, im = row(s, 0, c), row(s, 1, c)
                cos, sin = phase[:rows], phase[rows:]
                both_parts = jnp.concatenate([re * cos - im * sin, re * sin + im * cos], axis=0)
                mixed.append(both_parts.astype(jnp.bfloat16))
            found = [dot_lanes(value, pick_z(s, c)) for (s, c), value in zip(todo, mixed)]
            spans = [place(s, c) for s, c in todo]
            for n, (s, c) in enumerate(todo):
                span = pl.ds(spans[n] * pitch, both)
                if n % ahead == 0:
                    fresh = (c == 0) | (spans[n] != place(s, jnp.maximum(c - 1, 0)))
                    before_e, before_o = cells_e[span, :], cells_o[span, :]
                else:
                    fresh = spans[n] != spans[n - 1]
                    before_e, before_o = part_e, part_o
                part_e = found[n][:, :LANES] + jnp.where(fresh, 0.0, before_e)
                part_o = found[n][:, LANES:] + jnp.where(fresh, 0.0, before_o)
                cells_e[span, :] = part_e
                cells_o[span, :] = part_o
        return 0

    lax.fori_loop(0, turns, forward, 0)
    pltpu.make_async_copy(vloc, vloc, vloc_sem).wait()

    def strided(start):
        return pl.ds(start, half, stride=pitch)

    def beside(left, right):
        return jnp.concatenate([left, right], axis=1)

    def above(upper, lower):
        return jnp.concatenate([upper, lower], axis=0)

    def middle(turn, _):
        many = [turn * batch + j for j in range(batch)]
        starts = [k + odd * half * pitch for k in many for odd in range(2)]

        def pull(cells):
            return jnp.concatenate(
                [
                    beside(cells[strided(at), :], cells[strided(at + rows), :]).astype(jnp.bfloat16)
                    for at in starts
                ],
                axis=0,
            )

        even = dot(pull(cells_e), along_z(0))
        odd = dot(pull(cells_o), along_z(1))
        low, high = (even + odd).astype(jnp.bfloat16), (even - odd).astype(jnp.bfloat16)

        def stacked(n):
            part = slice(n * half, (n + 1) * half)
            return above(
                beside(low[part, :LANES], high[part, :LANES]),
                beside(low[part, LANES:], high[part, LANES:]),
            )

        sums, differences = [], []
        for j, k in enumerate(many):
            even = dot(along_x(0), stacked(2 * j))
            odd = dot(along_x(1), stacked(2 * j + 1))
            field = vloc[k]
            field = beside(field[:, :LANES], beside(field[:, half:], field[:, : LANES - half]))
            near, far = field[:half], field[half:]
            first = (even + odd) * above(near, near)
            second = (even - odd) * above(far, far)
            for table, value in ((along_x(2), first + second), (along_x(3), first - second)):
                back = dot(table, value.astype(jnp.bfloat16))
                total, change = back[:, :LANES] + back[:, LANES:], back[:, :LANES] - back[:, LANES:]
                sums.append(beside(total[:half], total[half:]).astype(jnp.bfloat16))
                differences.append(beside(change[:half], change[half:]).astype(jnp.bfloat16))
        even = dot(jnp.concatenate(sums, axis=0), along_z(2))
        odd = dot(jnp.concatenate(differences, axis=0), along_z(3))
        for n, at in enumerate(starts):
            part = slice(n * half, (n + 1) * half)
            cells_e[strided(at), :] = even[part, :LANES]
            cells_e[strided(at + rows), :] = even[part, LANES:]
            cells_o[strided(at), :] = odd[part, :LANES]
            cells_o[strided(at + rows), :] = odd[part, LANES:]
        return 0

    lax.fori_loop(0, planes // batch, middle, 0)

    def backward(turn, _):
        for base in range(0, blocks, group):
            todo = items(turn, base)
            found = []
            for s, c in todo:
                span = pl.ds(place(s, c) * pitch, both)
                value = beside(cells_e[span, :], cells_o[span, :]).astype(jnp.bfloat16)
                found.append(dot(value, pick_z(s, c)))
            for (s, c), part in zip(todo, found):
                phase = phases[s * chunks + c].astype(jnp.float32)
                re, im = part[:rows], part[rows:]
                cos, sin = phase[:rows], phase[rows:]
                result[pl.ds(s * 2 * chunks + c, 1), :] = jnp.sum(re * cos + im * sin, axis=0, keepdims=True)
                result[pl.ds((s * 2 + 1) * chunks + c, 1), :] = jnp.sum(im * cos - re * sin, axis=0, keepdims=True)
        return 0

    spare_span = pl.ds(spare * pitch, both)
    cells_e[spare_span, :] = jnp.zeros((both, LANES), jnp.float32)
    cells_o[spare_span, :] = jnp.zeros((both, LANES), jnp.float32)
    result[...] = jnp.zeros_like(result)
    lax.fori_loop(0, turns, backward, 0)
    rest = sums_ref[...]
    pieces = []
    for _ in range(3):
        pieces.append(rest.astype(jnp.bfloat16).astype(jnp.float32))
        rest = rest - pieces[-1]
    blank = jnp.zeros((5, LANES), jnp.float32)
    packed = [piece[:1] for piece in pieces] + [blank] + [piece[8:9] for piece in pieces] + [blank]
    packed = jnp.concatenate(packed, axis=0).astype(jnp.bfloat16)
    for s in range(blocks):
        outs[s][0 : 2 * chunks, :] = result[s * 2 * chunks : (s + 1) * 2 * chunks, :].astype(jnp.bfloat16)
        outs[s][2 * chunks :, :] = packed


def lattice(pays, sums, vloc, length, planes, chunks):
    blocks = len(pays)
    rows = round_up(planes, 8)
    tables = tables_of(length, planes, blocks)
    vmem = pl.BlockSpec(memory_space=pltpu.VMEM)
    return pl.pallas_call(
        functools.partial(lattice_kernel, length, planes, chunks, blocks),
        out_shape=[jax.ShapeDtypeStruct((2 * chunks + sums.shape[0], LANES), jnp.bfloat16)] * blocks,
        in_specs=[vmem] * (blocks + 1) + [pl.BlockSpec(memory_space=pl.ANY), vmem],
        out_specs=[vmem] * blocks,
        scratch_shapes=[
            pltpu.VMEM((blocks * 4 * chunks, LANES), jnp.float32),
            pltpu.VMEM((round_up((blocks * planes + 1) * (2 * rows + 1), 8), LANES), jnp.float32),
            pltpu.VMEM((round_up((blocks * planes + 1) * (2 * rows + 1), 8), LANES), jnp.float32),
            pltpu.VMEM((blocks * chunks, 2 * rows, LANES), jnp.bfloat16),
            pltpu.VMEM((planes, length, length), jnp.float32),
            pltpu.VMEM((blocks * 2 * chunks, LANES), jnp.float32),
            pltpu.VMEM((blocks * 8, LANES), jnp.int32),
            pltpu.SMEM((blocks * 8, LANES), jnp.int32),
            pltpu.SemaphoreType.DMA((1,)),
            pltpu.SemaphoreType.DMA,
        ],
        compiler_params=pltpu.CompilerParams(vmem_limit_bytes=48 * MIB),
        cost_estimate=cost(36.0),
        name="lattice",
    )(*pays, sums, vloc, tables)


def project_kernel(bands, *refs):
    beta_hbm, out_ref, beta_ref, sems = refs[-4:]
    (fetch,) = fetch_all(((beta_hbm, beta_ref),), sems)
    every = [ref[...].astype(jnp.float32) for ref in refs[:-4]]
    count = beta_ref.shape[1]
    rows = out_ref.shape[0] // 2
    pad = [jnp.zeros((rows - bands, every[0].shape[2]), jnp.float32)] if rows > bands else []
    re = jnp.concatenate([value[0] for value in every] + pad, axis=0)
    im = jnp.concatenate([value[1] for value in every] + pad, axis=0)
    fetch.wait()
    stack = jnp.concatenate([re, im], axis=0).astype(jnp.bfloat16)
    on_re, on_im = dot_lanes(beta_ref[0], stack), dot_lanes(beta_ref[1], stack)
    found = jnp.concatenate([on_re[:, :rows] + on_im[:, rows:], on_re[:, rows:] - on_im[:, :rows]], axis=1)
    out_ref[...] = jnp.zeros_like(out_ref)
    out_ref[:, :count] = found.T
    own_re, own_im = re[:1], im[:1]
    over = jnp.concatenate(
        [
            jnp.sum(re * own_re + im * own_im, axis=1, keepdims=True),
            jnp.sum(im * own_re - re * own_im, axis=1, keepdims=True),
        ],
        axis=0,
    )
    out_ref[...] = jnp.where(iota(out_ref.shape, 1) == count, over, out_ref[...])


def project(every, beta, bands):
    return pl.pallas_call(
        functools.partial(project_kernel, bands),
        out_shape=jax.ShapeDtypeStruct((2 * round_up(bands, 8), LANES), jnp.float32),
        in_specs=[pl.BlockSpec(memory_space=pltpu.VMEM)] * len(every) + [pl.BlockSpec(memory_space=pl.ANY)],
        scratch_shapes=[pltpu.VMEM(beta.shape, beta.dtype), pltpu.SemaphoreType.DMA((1,))],
        compiler_params=pltpu.CompilerParams(vmem_limit_bytes=16 * MIB),
        cost_estimate=cost(1.2),
        name="project",
    )(*every, beta)


def finish_kernel(length, planes, chunks, blocks, *refs):
    parts = refs[:blocks]
    slot_ref, gvec_ref, psi_ref, beta_ref, atoms_ref, hpsi_ref, spsi_ref = refs[blocks:]
    waves = slot_ref.shape[1]
    count = beta_ref.shape[1]
    total = parts[0][...].astype(jnp.float32)
    for part in parts[1:]:
        total = total + part[...].astype(jnp.float32)
    packed = total[2 * chunks :]
    half_size = packed.shape[0] // 2
    blank = jnp.zeros((half_size - 1, LANES), jnp.float32)
    sums = []
    for at in (0, half_size):
        sums += [packed[at : at + 1] + (packed[at + 1 : at + 2] + packed[at + 2 : at + 3]), blank]
    sums = jnp.concatenate(sums, axis=0)
    coef = jnp.dot(sums, atoms_ref[...], precision=lax.Precision.HIGHEST, preferred_element_type=jnp.float32)
    coef = coef.astype(jnp.bfloat16).astype(jnp.float32)
    d_re, d_im = coef[:1, :count], coef[half_size : half_size + 1, :count]
    q_re, q_im = coef[:1, LANES : LANES + count], coef[half_size : half_size + 1, LANES : LANES + count]
    none = jnp.zeros((4, count), jnp.float32)
    on_re = jnp.concatenate([d_re, d_im, q_re, q_im, none], axis=0).astype(jnp.bfloat16)
    on_im = jnp.concatenate([-d_im, d_re, -q_im, q_re, none], axis=0).astype(jnp.bfloat16)
    added = dot(on_re, beta_ref[0]) + dot(on_im, beta_ref[1])

    local = total[: 2 * chunks]
    turned = jnp.concatenate([local[:chunks].T, local[chunks:].T], axis=0).astype(jnp.bfloat16)
    x, y, z = cell_parts(gvec_ref[...], length)
    x = x + (lax.axis_index("pw") * planes).astype(jnp.float32)

    def fold(level):
        return jnp.where(level < length // 2, level, level - length)

    x, y, z = fold(x), fold(y), fold(z)
    kinetic = 4.0 * (x * x + y * y + z * z) / (length * length)
    slot = slot_ref[...]
    high = jnp.floor((slot + 0.5) * (1.0 / LANES))
    low = slot - high * LANES
    for tile in range(waves // LANES):
        span = slice(tile * LANES, (tile + 1) * LANES)
        at_high = where_bf16(iota((chunks, LANES), 0) == high[:, span], 1.0)
        rows = dot(turned, at_high)
        mine = iota((LANES, LANES), 0) == low[:, span]
        re = jnp.sum(jnp.where(mine, rows[:LANES], 0.0), axis=0, keepdims=True)
        im = jnp.sum(jnp.where(mine, rows[LANES:], 0.0), axis=0, keepdims=True)
        both = jnp.concatenate([re, im], axis=0)
        psi = psi_ref[:, span].astype(jnp.float32)
        hpsi_ref[:, span] = (both + kinetic[:, span] * psi + added[0:2, span]).astype(jnp.bfloat16)
        spsi_ref[:, span] = (psi + added[2:4, span]).astype(jnp.bfloat16)


def finish(parts, slot, index, psi, beta, atoms, length, planes, chunks):
    blocks = len(parts)
    return pl.pallas_call(
        functools.partial(finish_kernel, length, planes, chunks, blocks),
        out_shape=(
            jax.ShapeDtypeStruct(psi.shape, jnp.bfloat16),
            jax.ShapeDtypeStruct(psi.shape, jnp.bfloat16),
        ),
        compiler_params=pltpu.CompilerParams(vmem_limit_bytes=16 * MIB),
        cost_estimate=cost(2.1),
        name="finish",
    )(*parts, slot, index, psi, beta, atoms)


def gram_kernel(waves, bands, count, *refs):
    atoms_ref, gram_ref = refs[-2:]
    sums = refs[0][...]
    for ref in refs[1:-2]:
        sums = sums + ref[...]
    half_size = sums.shape[0] // 2
    coef = jnp.dot(sums, atoms_ref[...], precision=lax.Precision.HIGHEST, preferred_element_type=jnp.float32)
    coef = coef.astype(jnp.bfloat16).astype(jnp.float32)
    own_re, own_im = sums[:1], sums[half_size : half_size + 1]
    each_re, each_im = coef[:half_size, LANES:], coef[half_size:, LANES:]
    over = iota((half_size, LANES), 1) == count
    gram_re = own_re * each_re + own_im * each_im + jnp.where(over, sums[:half_size], 0.0)
    gram_im = own_re * each_im - own_im * each_re + jnp.where(over, sums[half_size:], 0.0)
    slot_at = lax.broadcasted_iota(jnp.int32, (half_size, bands), 0)
    if doubles(bands):
        turn = lax.axis_index("band")
        for place, step in enumerate(doubling_steps(bands)):
            turn = turn ^ (((slot_at >> place) & 1) * step)
    else:
        turn = lax.axis_index("band") - slot_at
        turn = jnp.where(turn < 0, turn + bands, turn)
    here = turn == lax.broadcasted_iota(jnp.int32, (half_size, bands), 1)
    here = here & (lax.broadcasted_iota(jnp.int32, (half_size, bands), 0) < bands)
    for n, value in enumerate((gram_re, gram_im)):
        value = jnp.sum(value, axis=1, keepdims=True)
        value = jnp.sum(jnp.where(here, value, 0.0), axis=0, keepdims=True)
        gram_ref[n : n + 1, :] = value * (1.0 / (waves))


def gram_row(parts, atoms, waves, bands, count):
    return pl.pallas_call(
        functools.partial(gram_kernel, waves, bands, count),
        out_shape=jax.ShapeDtypeStruct((2, bands), jnp.float32),
        compiler_params=pltpu.CompilerParams(vmem_limit_bytes=16 * MIB),
        cost_estimate=cost(0.7),
        name="gram_row",
    )(*parts, atoms)


def swap(value, axis, step):
    size = lax.axis_size(axis)
    return lax.ppermute(value, axis, [(k, k ^ step) for k in range(size)])


def doubles(size):
    return size & (size - 1) == 0


def doubling_steps(size):
    steps = [1 << place for place in range(size.bit_length() - 1)]
    return steps[:1] + steps[:0:-1]


def from_blocks(value, axis):
    size = lax.axis_size(axis)
    found = {0: value}
    step = size // 2
    while step:
        found.update({s + step: swap(found[s], axis, step) for s in list(found)})
        step //= 2
    return [found[s] for s in range(size)]


def from_bands_early(value, axis, after):
    size = lax.axis_size(axis)
    if not doubles(size):
        pairs = [[(k, (k + s) % size) for k in range(size)] for s in range(1, size)]
        held = [value] + [lax.ppermute(value, axis, pair) for pair in pairs]
        return [part[:, None] for part in held]
    held = [value[:, None]]
    for step in doubling_steps(size)[:-1]:
        if len(held) == 1:
            other = swap(value, axis, step)
            other, _ = lax.optimization_barrier((other, after))
            held.append(other[:, None])
        else:
            joined = jnp.concatenate(held, axis=1)
            held = [joined, swap(joined, axis, step)]
    return held


def from_bands_late(held, axis):
    size = lax.axis_size(axis)
    if size == 1 or not doubles(size):
        return held
    joined = jnp.concatenate(held, axis=1)
    return [joined, swap(joined, axis, doubling_steps(size)[-1])]


def atom_blocks(matrix):
    atoms, each = matrix.shape[0], matrix.shape[1]
    same = jnp.eye(atoms, dtype=matrix.dtype)[:, None, :, None]
    square = (same * jnp.transpose(matrix, (0, 2, 1))[:, :, None, :]).reshape(atoms * each, atoms * each)
    return jnp.pad(square, ((0, LANES - atoms * each), (0, LANES - atoms * each)))


def on_device(psi, gvec_index, vloc, beta, dmat, qmat):
    length = vloc.shape[0]
    planes = vloc.shape[1]
    width = psi.shape[2]
    blocks = lax.axis_size("pw")
    bands = lax.axis_size("band")
    chunks = round_up(width // LANES + planes, 16)
    index = gvec_index.reshape(1, width)
    mine = psi.reshape(2, width)
    pay, slot = group_waves(index, mine, length, planes, chunks)
    pays = from_blocks(pay, "pw")
    early = from_bands_early(mine, "band", pay)
    later, _ = lax.optimization_barrier((mine, pay))
    outs = lattice(pays, project([later[:, None]], beta, 1), vloc, length, planes, chunks)
    parts = [outs[0]] + [swap(outs[s], "pw", s) for s in range(1, blocks)]
    dmat, qmat, early, _ = lax.optimization_barrier((dmat, qmat, early, outs[0]))
    every = from_bands_late(early, "band")
    atoms = jnp.concatenate([atom_blocks(dmat), atom_blocks(qmat)], axis=1)
    hpsi, spsi = finish(parts, slot, index, mine, beta, atoms, length, planes, chunks)
    sums = project(every, beta, bands)
    sums = [sums] + [swap(sums, "pw", s) for s in range(1, blocks)]
    gram = gram_row(sums, atoms, width * blocks, bands, beta.shape[1])
    return (hpsi.reshape(2, 1, width), spsi.reshape(2, 1, width), gram.reshape(2, 1, bands))


def solution(mesh):
    in_specs = (P(None, "band", "pw"), P("pw"), P(None, "pw", None), P(None, None, "pw"), P(), P())
    out_specs = (P(None, "band", "pw"), P(None, "band", "pw"), P(None, "band", None))
    return jax.shard_map(
        on_device, mesh=mesh, in_specs=in_specs, out_specs=out_specs, check_vma=False
    )
```
